32 devices in a mesh: side: 2 (over y), group: 4 (over z), cuts: 4 (over x, core).
Axes of the slice: x: 2, y: 2, z: 4, core: 2. Of those that a mesh axis runs over, the one named last changes fastest.
Arguments:
- queries: bfloat16 [64, 4096], P('group', ('side', 'cuts')), may hold values from -8 to 8
- cache_keys: bfloat16 [64, 8, 64, 512], P('group', ('side', 'cuts')), may hold values from -8 to 8
- cache_values: bfloat16 [64, 8, 64, 512], P('group', ('side', 'cuts')), may hold values from -6 to 6
- new_keys: bfloat16 [64, 512], P('group', ('side', 'cuts')), may hold values from -8 to 8
- new_values: bfloat16 [64, 512], P('group', ('side', 'cuts')), may hold values from -6 to 6
- lengths: int32 [64], P('group'), may hold values from 1 to 512, as said below
- head_sinks: float32 [64], P(('side', 'cuts')), may hold values from 0 to 6
- attn_proj: bfloat16 [4096, 2880], P(('side', 'cuts'), 'group'), may hold values from -0.625 to 0.625
- residual_in: bfloat16 [64, 2880], P('group'), may hold values from -8 to 8
- norm_gain: float32 [2880], replicated, may hold values from 0.25 to 1.75
- router: bfloat16 [2880, 32], replicated, may hold values from -0.109375 to 0.109375
- expert_routes: int32 [64, 4], P('group'), may hold values from 0 to 31, all different within a row; in each aligned block of 16 rows (0 to 15, 16 to 31, ...) at most 4 rows name the same one
- expert_gate: bfloat16 [2880, 92160], P(None, ('side', 'group', 'cuts')), may hold values from -0.109375 to 0.109375
- expert_up: bfloat16 [2880, 92160], P(None, ('side', 'group', 'cuts')), may hold values from -0.109375 to 0.109375
- expert_down: bfloat16 [92160, 2880], P(('side', 'group', 'cuts')), may hold values from -0.109375 to 0.109375
- adapter_in: bfloat16 [2880, 32], replicated, may hold values from -0.109375 to 0.109375
- adapter_gate: bfloat16 [32, 92160], P(None, ('side', 'group', 'cuts')), may hold values from -1 to 1
- adapter_up: bfloat16 [32, 92160], P(None, ('side', 'group', 'cuts')), may hold values from -1 to 1
Outputs:
- hidden_out: bfloat16 [64, 2880], P('group', 'cuts')
The draws below stay inside these ranges and needn't reach their ends.
Inputs may be any that keep to these rules, and one draw needn't show every extreme that they name: `expert_routes`: the 16 requests of one index of group name any one expert at most 4 times, a bound that some block reaches. `lengths`: some request has all 512 positions valid.
All inputs are finite; a program needn't handle non-finite values.
Results may differ from the reference program's by a relative error of at most 0.02.
Values may be sent and summed in bfloat16 or wider, within the bound.
A program may use at most 128 MiB of HBM per device.

```python
import math
import jax
import jax.numpy as jnp
import numpy as np
from jax import lax

D = 2880
FF = 2880
EXPERTS = 32
TOPK = 4
HEADS = 64
KV_HEADS = 8
HEAD_DIM = 64
RANK = 32
CACHE = 512
REQ_DEV = 16
CAP = 4
REQUESTS = 64
N_GROUP = 4


def drawn_floats(key, shape):
    return jnp.clip(jax.random.normal(key, shape, jnp.float32), -6.0, 6.0)


def draw_queries(key, part):
    values = drawn_floats(jax.random.fold_in(key, 11), (REQUESTS, HEADS, HEAD_DIM))
    return values.reshape(REQUESTS, HEADS * HEAD_DIM).astype(jnp.bfloat16)


def draw_cache_keys(key, part):
    values = drawn_floats(jax.random.fold_in(key, 12), (REQUESTS, KV_HEADS, HEAD_DIM, CACHE))
    return values.astype(jnp.bfloat16)


def draw_new_keys(key, part):
    values = drawn_floats(jax.random.fold_in(key, 13), (REQUESTS, KV_HEADS, HEAD_DIM))
    return values.reshape(REQUESTS, KV_HEADS * HEAD_DIM).astype(jnp.bfloat16)


def draw_lengths(key, part):
    drawn = jax.random.randint(jax.random.fold_in(key, 31), (REQUESTS,), 1, CACHE + 1)
    full_at = jax.random.randint(jax.random.fold_in(key, 32), (), 0, REQUESTS)
    return jnp.where(jnp.arange(REQUESTS) == full_at, CACHE, drawn).astype(jnp.int32)


def draw_residual_in(key, part):
    values = 0.5 * jnp.clip(jax.random.normal(jax.random.fold_in(key, 44), (REQUESTS, D), jnp.float32), -6.0, 6.0)
    return values.astype(jnp.bfloat16)


def steps_of(rng, shape, shards, smallest, top_value):
    loudness, own = 1.0, jax.random.fold_in(rng, 6)
    for dim, shards_of in shards:
        steps = jnp.exp(jax.random.uniform(jax.random.fold_in(own, dim), (shards_of,), jnp.float32, smallest / len(shards), top_value / len(shards)))
        loudness = loudness * jnp.repeat(steps, shape[dim] // shards_of).reshape([-1 if axis == dim else 1 for axis in range(len(shape))])
    return loudness


def shared_out(own_key, own, number, rows, number_of, top, limit, lean):
    ranking = jax.random.permutation(own_key, number_of)
    packed, common = shares(number_of, rows * top, limit, lean, True), shares(number_of, rows * top, limit, lean, False)
    places = jnp.arange(number_of)

    def named(sizes, turn):
        used = int((sizes > 0).sum())
        fixed = max(1, used // 4)
        moved = fixed + (places - fixed + turn * (used - fixed)) % max(1, number_of - fixed)
        return jnp.zeros((number_of,), jnp.int32).at[ranking[jnp.where(places < fixed, places, moved)]].set(jnp.asarray(sizes, jnp.int32))

    sizes = jnp.where(number % 4 == 0, named(packed, number // 4), named(common, number - number // 4 - 1))
    mixed = jax.random.permutation(jax.random.fold_in(own, 3), number_of)
    source_of, sink = mixed[0:number_of // 2 * 2:2], mixed[1:number_of // 2 * 2:2]
    margin = jnp.minimum(sizes[source_of] - 1, limit - sizes[sink]) // 2
    margin = jnp.where((source_of == ranking[0]) | (sink == ranking[0]) | (sizes[sink] == 0), 0, jnp.maximum(margin, 0))
    moved = jax.random.randint(jax.random.fold_in(own, 4), (number_of // 2,), 0, 1 << 20) % (margin + 1)
    sizes = sizes.at[source_of].add(-moved).at[sink].add(moved)
    labels = jnp.searchsorted(jnp.cumsum(sizes), jnp.arange(rows * top), side="right").astype(jnp.int32)
    table = labels.reshape(top, rows).T
    table = table[jax.random.permutation(jax.random.fold_in(own, 1), rows)]
    turn = jax.random.randint(jax.random.fold_in(own, 2), (rows, 1), 0, top)
    return jnp.take_along_axis(table, (jnp.arange(top)[None, :] + turn) % top, axis=1)


def shares(amount, total, most, skew, full):
    portions = [(1 << 20) // math.isqrt(grade ** skew) + 1 for grade in range(1, amount + 1)]
    largest = most if full else min(most, max(-(-total // amount), total * portions[0] // sum(portions)))
    least = 1 if total - largest >= amount - 1 else 0
    holding, spare = [largest] + [least] * (amount - 1), total - largest - least * (amount - 1)
    while spare > 0:
        candidates = [i for i in range(1, amount) if holding[i] < largest] or [i for i in range(1, amount) if holding[i] < most]
        mass, remaining = sum([portions[i] for i in candidates]), spare
        for i in candidates:
            extra = min(most - holding[i], max(1, remaining * portions[i] // mass), spare)
            holding[i] = holding[i] + extra
            spare = spare - extra
    return np.array(holding)


def gaussian(stream_key, shape, spread, most, split=(), held_as=jnp.bfloat16):
    values = jax.random.normal(stream_key, shape, jnp.float32) * spread
    if len(split) > 0:
        values = steps_of(stream_key, shape, split, -0.22, 0.18) * values
    return jnp.clip(values, min=-most, max=most).astype(held_as)


def setup_inputs(seed: int = 0) -> dict:
    seeds = jax.random.split(jax.random.key(seed), 19)
    queries = draw_queries(jax.random.fold_in(seeds[18], 71), 0)
    cache_keys = draw_cache_keys(jax.random.fold_in(seeds[18], 71), 0)
    cache_values = gaussian(seeds[2], (REQUESTS, KV_HEADS, HEAD_DIM, CACHE), 1.0, 6.0, ((0, 4), (1, 8)))
    new_keys = draw_new_keys(jax.random.fold_in(seeds[18], 71), 0)
    new_values = gaussian(seeds[4], (REQUESTS, KV_HEADS * HEAD_DIM), 1.0, 6.0, ((0, 4), (1, 8)))
    lengths = draw_lengths(jax.random.fold_in(seeds[18], 71), 0)
    head_sinks = jnp.clip(6.0 * jax.random.uniform(seeds[6], (HEADS,), jnp.float32) ** steps_of(seeds[6], (HEADS,), ((0, 8),), -0.2, 0.2), 0.0, 6.0)
    attn_proj = gaussian(seeds[7], (HEADS * HEAD_DIM, D), 0.1, 0.625, ((0, 8), (1, 4)))
    residual_in = draw_residual_in(jax.random.fold_in(seeds[18], 71), 0)
    norm_gain = jnp.clip(1.0 + 0.15 * jax.random.normal(seeds[9], (D,), jnp.float32), 0.25, 1.75)
    router = gaussian(seeds[10], (D, EXPERTS), D ** -0.5, 0.109375)
    expert_routes_keys = jax.random.split(jax.random.fold_in(seeds[11], 1), REQUESTS // REQ_DEV)
    expert_routes_turns = jax.random.permutation(jax.random.fold_in(seeds[11], 3), REQUESTS // REQ_DEV)
    expert_routes = jax.vmap(lambda own, number: shared_out(jax.random.fold_in(seeds[11], 2), own, number, REQ_DEV, EXPERTS, TOPK, CAP, 2))(expert_routes_keys, expert_routes_turns).reshape((REQUESTS, TOPK))
    expert_gate = gaussian(seeds[12], (D, EXPERTS * FF), D ** -0.5, 0.109375, ((1, 32),))
    expert_up = gaussian(seeds[13], (D, EXPERTS * FF), D ** -0.5, 0.109375, ((1, 32),))
    expert_down = gaussian(seeds[14], (EXPERTS * FF, D), FF ** -0.5, 0.109375, ((0, 32),))
    adapter_in = gaussian(seeds[15], (D, RANK), D ** -0.5, 0.109375)
    adapter_gate = gaussian(seeds[16], (RANK, EXPERTS * FF), RANK ** -0.5, 1.0, ((1, 32),))
    adapter_up = gaussian(seeds[17], (RANK, EXPERTS * FF), RANK ** -0.5, 1.0, ((1, 32),))
    return dict(queries=queries, cache_keys=cache_keys, cache_values=cache_values, new_keys=new_keys, new_values=new_values, lengths=lengths, head_sinks=head_sinks, attn_proj=attn_proj, residual_in=residual_in, norm_gain=norm_gain, router=router, expert_routes=expert_routes, expert_gate=expert_gate, expert_up=expert_up, expert_down=expert_down, adapter_in=adapter_in, adapter_gate=adapter_gate, adapter_up=adapter_up)


def attention_rows(queries, cache_keys, cache_values, new_keys, new_values, lengths, head_sinks):
    req_count = queries.shape[0]
    kv_count = cache_keys.shape[1]
    head_dim = cache_keys.shape[2]
    cache_len = cache_keys.shape[3]
    head_count = head_sinks.shape[0]
    group_size = head_count // kv_count
    query_rows = queries.reshape(req_count, kv_count, group_size, head_dim).astype(jnp.float32)
    fresh_key = new_keys.reshape(req_count, kv_count, head_dim).astype(jnp.float32)
    fresh_value = new_values.reshape(req_count, kv_count, head_dim).astype(jnp.float32)
    scaling = 1.0 / math.sqrt(head_dim)
    scores = jnp.einsum('rkgd,rkdl->rkgl', query_rows, cache_keys.astype(jnp.float32)) * scaling
    own_score = jnp.einsum('rkgd,rkd->rkg', query_rows, fresh_key) * scaling
    validity = lax.broadcasted_iota(jnp.int32, (req_count, 1, 1, cache_len), 3) < lengths[:, None, None, None]
    scores = jnp.where(validity, scores, -1e+30)
    sink_logit = head_sinks.reshape(1, kv_count, group_size)
    highest = jnp.maximum(jnp.maximum(lax.optimization_barrier(jnp.max(scores, axis=3)), own_score), sink_logit)
    exp_terms = jnp.where(validity, jnp.exp(scores - highest[..., None]), 0.0)
    own_term = jnp.exp(own_score - highest)
    denominator = lax.optimization_barrier(jnp.sum(exp_terms, axis=3)) + own_term + jnp.exp(sink_logit - highest)
    attn_probs = (exp_terms / denominator[..., None]).astype(jnp.bfloat16)
    own_prob = (own_term / denominator).astype(jnp.bfloat16)
    attn_mix = jnp.einsum('rkgl,rkdl->rkgd', attn_probs.astype(jnp.float32), cache_values.astype(jnp.float32))
    attn_mix = attn_mix + own_prob.astype(jnp.float32)[..., None] * fresh_value[:, :, None, :]
    return attn_mix.astype(jnp.bfloat16).reshape(req_count, head_count * head_dim)

def reference(queries, cache_keys, cache_values, new_keys, new_values, lengths, head_sinks, attn_proj, residual_in, norm_gain, router, expert_routes, expert_gate, expert_up, expert_down, adapter_in, adapter_gate, adapter_up):
    attn_out = attention_rows(queries, cache_keys, cache_values, new_keys, new_values, lengths, head_sinks)
    projected = jnp.dot(attn_out, attn_proj, preferred_element_type=jnp.float32)
    middle = residual_in.astype(jnp.float32) + projected
    inverse = lax.rsqrt(lax.optimization_barrier(jnp.mean(middle * middle, axis=1, keepdims=True)) + 1e-05)
    normed = (middle * inverse * norm_gain).astype(jnp.bfloat16)
    logits = jnp.dot(normed, router, preferred_element_type=jnp.float32)
    picked = jnp.take_along_axis(logits, expert_routes, axis=1)
    raw_gate = jax.nn.sigmoid(picked)
    gate_weights = raw_gate / lax.optimization_barrier(jnp.sum(raw_gate, axis=1, keepdims=True))
    low_code = jnp.dot(normed, adapter_in, preferred_element_type=jnp.float32).astype(jnp.bfloat16)
    capacity = N_GROUP * CAP

    def one_expert(moe_sum, expert):
        matched = expert_routes == expert
        weight_rows = lax.optimization_barrier(jnp.sum(jnp.where(matched, gate_weights, 0.0), axis=1))
        member = jnp.any(matched, axis=1)
        picks = jnp.nonzero(member, size=capacity, fill_value=0)[0].astype(jnp.int32)
        live = jnp.arange(capacity) < jnp.sum(member.astype(jnp.int32))
        row_weight = jnp.where(live, weight_rows[picks], 0.0)
        rows_in = normed[picks]
        rows_code = low_code[picks]
        first_col = (expert * FF).astype(jnp.int32)
        pre_gate = jnp.dot(rows_in, lax.dynamic_slice_in_dim(expert_gate, first_col, FF, 1), preferred_element_type=jnp.float32)
        pre_gate = pre_gate + jnp.dot(rows_code, lax.dynamic_slice_in_dim(adapter_gate, first_col, FF, 1), preferred_element_type=jnp.float32)
        pre_up = jnp.dot(rows_in, lax.dynamic_slice_in_dim(expert_up, first_col, FF, 1), preferred_element_type=jnp.float32)
        pre_up = pre_up + jnp.dot(rows_code, lax.dynamic_slice_in_dim(adapter_up, first_col, FF, 1), preferred_element_type=jnp.float32)
        activated = ((pre_up + 1.0) * pre_gate * jax.nn.sigmoid(1.702 * pre_gate)).astype(jnp.bfloat16)
        out_rows = jnp.dot(activated, lax.dynamic_slice_in_dim(expert_down, first_col, FF, 0), preferred_element_type=jnp.float32)
        moe_sum = moe_sum.at[picks].add(out_rows * row_weight[:, None])
        return (moe_sum, None)
    moe, unused = lax.scan(one_expert, jnp.zeros((REQUESTS, D), jnp.float32), jnp.arange(EXPERTS, dtype=jnp.int32))
    return (middle + moe).astype(jnp.bfloat16)
```

```python
import functools
import math

import jax
import jax.numpy as jnp
from jax import lax
from jax.experimental import pallas as pl
from jax.experimental.pallas import tpu as pltpu
from jax.sharding import PartitionSpec as P

FF = 2880
CAP = 4


epsilon = 1e-05


def attention_rows(queries, cache_keys, cache_values, new_keys, new_values, lengths, head_sinks):
    req_count = queries.shape[0]
    kv_count = cache_keys.shape[1]
    head_dim = cache_keys.shape[2]
    cache_len = cache_keys.shape[3]
    head_count = head_sinks.shape[0]
    group_size = head_count // kv_count
    query_rows = queries.reshape(req_count, kv_count, group_size, head_dim)
    fresh_key = new_keys.reshape(req_count, kv_count, head_dim)
    fresh_value = new_values.reshape(req_count, kv_count, head_dim)
    scaling = 1.0 / math.sqrt(head_dim)
    scores = (
        jnp.einsum("rkgd,rkdl->rkgl", query_rows, cache_keys, preferred_element_type=jnp.float32)
        * scaling
    )
    own_score = (
        jnp.einsum("rkgd,rkd->rkg", query_rows, fresh_key, preferred_element_type=jnp.float32)
        * scaling
    )
    validity = (
        lax.broadcasted_iota(jnp.int32, (req_count, 1, 1, cache_len), 3)
        < lengths[:, None, None, None]
    )
    scores = jnp.where(validity, scores, -1e30)
    sink_logit = head_sinks.reshape(1, kv_count, group_size)
    highest = jnp.maximum(jnp.maximum(jnp.max(scores, axis=3), own_score), sink_logit)
    exp_terms = jnp.where(validity, jnp.exp(scores - highest[..., None]), 0.0)
    own_term = jnp.exp(own_score - highest)
    denominator = jnp.sum(exp_terms, axis=3) + own_term + jnp.exp(sink_logit - highest)
    attn_probs = (exp_terms / denominator[..., None]).astype(jnp.bfloat16)
    own_prob = (own_term / denominator).astype(jnp.bfloat16)
    attn_mix = jnp.einsum(
        "rkgl,rkdl->rkgd", attn_probs, cache_values, preferred_element_type=jnp.float32
    )
    attn_mix = (
        attn_mix
        + own_prob.astype(jnp.float32)[..., None] * fresh_value.astype(jnp.float32)[:, :, None, :]
    )
    return attn_mix.astype(jnp.bfloat16).reshape(req_count, head_count * head_dim)


def routing_matrix(expert_table, expert_routes, slot_pos, weights):
    slot_total = CAP
    matched = (expert_routes[None, None, :, :] == expert_table[:, :, None, None]).astype(
        jnp.float32
    )
    slot_hot = (
        slot_pos[:, :, None] == lax.broadcasted_iota(jnp.int32, (1, 1, slot_total), 2)
    ).astype(jnp.float32)
    return jnp.einsum(
        "gjrk,rkc->gjcr",
        matched * weights[None, None, :, :],
        slot_hot,
        precision=lax.Precision.HIGHEST,
    )

MESH = pl.DeviceIdType.MESH
F32 = jnp.float32
BF16 = jnp.bfloat16
QUARTERS = 4


def idiv(value, by):
    if by & (by - 1) == 0:
        return lax.shift_right_logical(value, jnp.full_like(value, by.bit_length() - 1))
    return lax.div(value, jnp.full_like(value, by))


def imod(value, by):
    return value - idiv(value, by) * by


def iota(shape, dim):
    return lax.broadcasted_iota(jnp.int32, shape, dim)


def hot(condition):
    return jnp.where(condition, 1.0, 0.0)


def dot(a, b):
    return jnp.dot(a, b, preferred_element_type=F32)


def dot_nt(a, b):
    return lax.dot_general(a, b, (((1,), (1,)), ((), ())), preferred_element_type=F32)


def swap_digits(outer, inner, tail, dtype):
    size = outer * inner * tail
    row, col = iota((size, size), 0), iota((size, size), 1)
    r_in, r_out, r_tail = idiv(row, outer * tail), imod(idiv(row, tail), outer), imod(row, tail)
    wanted = (r_out * inner + r_in) * tail + r_tail
    return hot(col == wanted).astype(dtype)


def layer_kernel(
    sizes,
    len_ref,
    sink_ref,
    q_hbm,
    nk_hbm,
    nv_hbm,
    ck_hbm,
    cv_hbm,
    proj_hbm,
    resid_hbm,
    gain_hbm,
    router_hbm,
    routes_hbm,
    wg_hbm,
    wu_hbm,
    wd_hbm,
    ain_hbm,
    ag_hbm,
    au_hbm,
    out_ref,
    q_v,
    nk_v,
    nv_v,
    ck_v,
    cv_v,
    proj_v,
    resid_v,
    gain_v,
    router_v,
    routes_v,
    wg_v,
    wu_v,
    wd_v,
    ain_v,
    ag_v,
    au_v,
    agb,
    pb,
    rb,
    sc,
    rc,
    nst,
    mid,
    sd,
    xd,
    xp,
    act,
    yb,
    yq,
    se,
    re,
    in_sem,
    w_sem,
    send_a,
    recv_a,
    send_b,
    recv_b,
    send_c,
    recv_c,
    send_d,
    recv_d,
    send_e,
    recv_e,
):
    n_side, n_group, n_cuts, reqs, heads, hd, width, ff, blk, experts, topk, half = sizes
    plane = n_side * n_cuts
    total = plane * n_group
    part = blk // QUARTERS
    s = lax.axis_index("side")
    g = lax.axis_index("group")
    c = lax.axis_index("cuts")
    d = s * n_cuts + c
    me = (s * n_group + g) * n_cuts + c

    def at(side, group, cut):
        return {"side": side, "group": group, "cuts": cut}

    first = [(q_hbm, q_v), (nk_hbm, nk_v), (nv_hbm, nv_v), (ck_hbm, ck_v), (cv_hbm, cv_v)]
    second = [
        (proj_hbm, proj_v),
        (resid_hbm, resid_v),
        (gain_hbm, gain_v),
        (routes_hbm, routes_v),
        (router_hbm, router_v),
        (ain_hbm, ain_v),
        (ag_hbm, ag_v),
        (au_hbm, au_v),
    ]
    small = [
        pltpu.make_async_copy(a, b, in_sem.at[i]) for i, (a, b) in enumerate(first + second)
    ]
    for copy in small:
        copy.start()
    rows = width // n_group
    weights = []
    for m, (a, b) in enumerate(((wg_hbm, wg_v), (wu_hbm, wu_v), (wd_hbm, wd_v))):
        weights.append(
            [
                pltpu.make_async_copy(
                    a.at[pl.ds(i * rows, rows)], b.at[pl.ds(i * rows, rows)], w_sem.at[m, i]
                )
                for i in range(n_group)
            ]
        )
        for copy in weights[-1]:
            copy.start()

    barrier = pltpu.get_barrier_semaphore()

    def greet(i, carry):
        other = lax.rem(me + i, total)
        pl.semaphore_signal(
            barrier,
            inc=1,
            device_id=at(
                lax.div(other, n_group * n_cuts),
                lax.rem(lax.div(other, n_cuts), n_group),
                lax.rem(other, n_cuts),
            ),
            device_id_type=MESH,
        )
        return carry

    lax.fori_loop(1, total, greet, 0)

    pb[...] = jnp.zeros_like(pb)
    nst[...] = jnp.zeros_like(nst)
    sc[...] = jnp.zeros_like(sc)
    yq[...] = jnp.zeros_like(yq)

    n_rows = reqs * heads
    for copy in small[:4]:
        copy.wait()
    q = q_v[...]
    q_stack = jnp.concatenate([q[:, h * hd : (h + 1) * hd] for h in range(heads)], axis=0)
    q_rows = dot(swap_digits(heads, reqs, 1, BF16), q_stack)
    spread = hot(
        idiv(iota((n_rows, reqs), 0), heads) == iota((n_rows, reqs), 1)
    ).astype(BF16)
    nk_rows = dot(spread, nk_v[...])
    scaling = 1.0 / math.sqrt(hd)
    cache = ck_v.shape[2]
    place = iota((heads, cache), 1)
    scores = []
    for r in range(reqs):
        raw = dot(q_rows[r * heads : (r + 1) * heads].astype(BF16), ck_v[r]) * scaling
        scores.append(jnp.where(place < len_ref[r], raw, -1e30))
    scores = jnp.concatenate(scores, axis=0)
    own = jnp.sum(q_rows * nk_rows, axis=1, keepdims=True) * scaling
    head_of = iota((heads, 1), 0)
    sink = jnp.zeros((heads, 1), F32)
    for h in range(heads):
        sink = jnp.where(head_of == h, sink_ref[h], sink)
    sink = jnp.concatenate([sink] * reqs, axis=0)
    top = jnp.maximum(jnp.maximum(jnp.max(scores, axis=1, keepdims=True), own), sink)
    terms = jnp.exp(scores - top)
    own_term = jnp.exp(own - top)
    denominator = jnp.sum(terms, axis=1, keepdims=True) + own_term + jnp.exp(sink - top)
    probs = terms / denominator
    own_prob = (own_term / denominator).astype(BF16).astype(F32)
    small[4].wait()
    nv_rows = dot(spread, nv_v[...])
    mixed = jnp.concatenate(
        [
            dot_nt(probs[r * heads : (r + 1) * heads].astype(BF16), cv_v[r])
            for r in range(reqs)
        ],
        axis=0,
    )
    mixed = (mixed + own_prob * nv_rows).astype(BF16)
    mixed = dot(swap_digits(reqs, heads, 1, BF16), mixed)
    agb[g] = jnp.concatenate(
        [mixed[h * reqs : (h + 1) * reqs] for h in range(heads)], axis=1
    ).astype(BF16)

    pl.semaphore_wait(barrier, total - 1)

    sends = []
    for i in range(1, n_group):
        to = lax.rem(g + i, n_group)
        copy = pltpu.make_async_remote_copy(
            src_ref=agb.at[g],
            dst_ref=agb.at[g],
            send_sem=send_a.at[to],
            recv_sem=recv_a.at[g],
            device_id=at(s, to, c),
            device_id_type=MESH,
        )
        copy.start()
        sends.append(copy)

    for copy in small[5:]:
        copy.wait()
    routes = routes_v[...]
    lane_e = iota((reqs, experts), 1)
    chosen = [hot(routes[:, j : j + 1] == lane_e) for j in range(topk)]
    member = functools.reduce(jnp.add, chosen)
    earlier = hot(iota((reqs, reqs), 1) < iota((reqs, reqs), 0)).astype(BF16)
    before = dot(earlier, member.astype(BF16))
    n_pack = n_group * n_group * CAP
    row_e = iota((n_pack, experts), 0)
    dest = (s * n_group + idiv(row_e, n_group * CAP)) * n_cuts + c
    picks = hot(iota((n_pack, experts), 1) == dest).astype(BF16)
    is_member = dot_nt(picks, member.astype(BF16))
    is_before = dot_nt(picks, before.astype(BF16))
    slot_of = imod(iota((n_pack, reqs), 0), CAP).astype(F32)
    placed = is_member * hot(is_before == slot_of)
    n_stack = n_group * reqs
    tile_out = hot(
        imod(iota((reqs, n_stack), 1), reqs) == iota((reqs, n_stack), 0)
    ).astype(BF16)
    place_rows = dot(placed.astype(BF16), tile_out)
    same_blk = imod(idiv(iota((n_pack, n_stack), 0), CAP), n_group) == idiv(
        iota((n_pack, n_stack), 1), reqs
    )
    place_rows = jnp.where(same_blk, place_rows, 0.0).astype(BF16)
    resid = resid_v[...]

    for i in range(1, n_group):
        peer = lax.rem(g + i, n_group)
        pltpu.make_async_remote_copy(
            src_ref=agb.at[g],
            dst_ref=agb.at[peer],
            send_sem=send_a.at[peer],
            recv_sem=recv_a.at[peer],
            device_id=at(s, peer, c),
            device_id_type=MESH,
        ).wait_recv()
    gathered = jnp.concatenate([agb[i] for i in range(n_group)], axis=0)
    pb[:, :blk] = dot(gathered, proj_v[...]).astype(BF16)

    for i in range(1, plane):
        to = lax.rem(d + i, plane)
        copy = pltpu.make_async_remote_copy(
            src_ref=pb.at[
                pl.ds(pl.multiple_of(lax.div(to, 2) * reqs, reqs), reqs),
                pl.ds(pl.multiple_of(lax.rem(to, 2) * half, half), half),
            ],
            dst_ref=rb.at[d],
            send_sem=send_b.at[to],
            recv_sem=recv_b.at[d],
            device_id=at(lax.div(to, n_cuts), g, lax.rem(to, n_cuts)),
            device_id_type=MESH,
        )
        copy.start()
        sends.append(copy)
    row_block, col_half = lax.div(d, 2), lax.rem(d, 2)
    total_block = pb[
        pl.ds(pl.multiple_of(row_block * reqs, reqs), reqs),
        pl.ds(pl.multiple_of(col_half * half, half), half),
    ].astype(F32)
    for i in range(1, plane):
        peer = lax.rem(d + i, plane)
        pltpu.make_async_remote_copy(
            src_ref=sc,
            dst_ref=rb.at[peer],
            send_sem=send_b.at[peer],
            recv_sem=recv_b.at[peer],
            device_id=at(lax.div(peer, n_cuts), g, lax.rem(peer, n_cuts)),
            device_id_type=MESH,
        ).wait_recv()
        total_block = total_block + rb[peer].astype(F32)
    summed = total_block.astype(BF16)
    sc[...] = summed

    for i in range(plane):
        to = lax.rem(d + i, plane)

        def send_sum(to=to):
            pltpu.make_async_remote_copy(
                src_ref=sc,
                dst_ref=rc.at[g, col_half],
                send_sem=send_c.at[to],
                recv_sem=recv_c.at[g, col_half],
                device_id=at(lax.div(to, n_cuts), row_block, lax.rem(to, n_cuts)),
                device_id_type=MESH,
            ).start()

        if i == 0:
            pl.when(row_block != g)(send_sum)

            @pl.when(row_block == g)
            def _():
                rc[g, col_half] = summed
        else:
            send_sum()

    def sums_from(i, h):
        pos = 2 * g + h
        return pltpu.make_async_remote_copy(
            src_ref=sc,
            dst_ref=rc.at[i, h],
            send_sem=send_c.at[0],
            recv_sem=recv_c.at[i, h],
            device_id=at(lax.div(pos, n_cuts), i, lax.rem(pos, n_cuts)),
            device_id_type=MESH,
        )

    squares = jnp.zeros((reqs, 1), F32)
    for i in range(n_group):
        for h in range(2):
            mine = jnp.logical_and(i == g, 2 * g + h == d)

            @pl.when(jnp.logical_not(mine))
            def _(i=i, h=h):
                sums_from(i, h).wait_recv()

    middles = []
    for i in range(n_group):
        projected = jnp.concatenate([rc[i, 0], rc[i, 1]], axis=1)[:, :blk].astype(F32)
        middle = resid[:, i * blk : (i + 1) * blk].astype(F32) + projected
        mid[i * reqs : (i + 1) * reqs, :] = middle
        squares = squares + jnp.sum(middle * middle, axis=1, keepdims=True)
        middles.append(middle)
    inverse = lax.rsqrt(squares / width + epsilon)
    gain = gain_v[...]
    for i in range(n_group):
        normed = (middles[i] * inverse * gain[:, i * blk : (i + 1) * blk]).astype(BF16)
        nst[i * reqs : (i + 1) * reqs, :blk] = normed

    packed = dot(place_rows, nst[...]).astype(BF16)
    pack = n_group * CAP
    for i in range(n_group):
        sd[i] = packed[i * pack : (i + 1) * pack]
    for i in range(1, n_group):
        to = lax.rem(g + i, n_group)
        copy = pltpu.make_async_remote_copy(
            src_ref=sd.at[to],
            dst_ref=xd.at[g],
            send_sem=send_d.at[to],
            recv_sem=recv_d.at[g],
            device_id=at(s, to, c),
            device_id_type=MESH,
        )
        copy.start()
        sends.append(copy)
    xd[g] = sd[g]

    logits = jnp.zeros((reqs, experts), F32)
    for i in range(n_group):
        logits = logits + dot(
            nst[i * reqs : (i + 1) * reqs, :blk], router_v[i * blk : (i + 1) * blk, :]
        )
    raw = [jax.nn.sigmoid(jnp.sum(hits * logits, axis=1, keepdims=True)) for hits in chosen]
    raw_sum = functools.reduce(jnp.add, raw)
    weight = functools.reduce(jnp.add, [hits * (x / raw_sum) for hits, x in zip(chosen, raw)])
    weight_hi = weight.astype(BF16)
    weight_lo = (weight - weight_hi.astype(F32)).astype(BF16)
    unit = QUARTERS * CAP
    wide = experts * unit
    widen = hot(idiv(iota((experts, wide), 1), unit) == iota((experts, wide), 0)).astype(BF16)
    slot_ok = dot(before.astype(BF16), widen) == imod(iota((reqs, wide), 1), CAP).astype(F32)
    quarter_of = imod(idiv(iota((reqs, wide), 1), CAP), QUARTERS)
    combine = []
    for value in (weight_hi, weight_lo):
        spread_w = jnp.where(slot_ok, dot(value, widen), 0.0)
        combine.append(
            jnp.concatenate(
                [jnp.where(quarter_of == i, spread_w, 0.0) for i in range(QUARTERS)], axis=0
            ).astype(BF16)
        )

    for i in range(1, n_group):
        peer = lax.rem(g + i, n_group)
        pltpu.make_async_remote_copy(
            src_ref=sd.at[peer],
            dst_ref=xd.at[peer],
            send_sem=send_d.at[peer],
            recv_sem=recv_d.at[peer],
            device_id=at(s, peer, c),
            device_id_type=MESH,
        ).wait_recv()
    arrived = jnp.concatenate([xd[i] for i in range(n_group)], axis=0)
    swap = swap_digits(n_group, n_group, CAP, BF16)
    xp[...] = dot(swap, arrived).astype(BF16)

    low = jnp.zeros((pack, ain_v.shape[1]), F32)
    for i in range(n_group):
        low = low + dot(xp[i * pack : (i + 1) * pack, :blk], ain_v[i * blk : (i + 1) * blk, :])
    low = low.astype(BF16)

    for copies in weights[:2]:
        for copy in copies:
            copy.wait()

    def hidden_cols(cols):
        pre_gate = dot(low, ag_v[:, cols])
        pre_up = dot(low, au_v[:, cols])
        for i in range(n_group):
            x = xp[i * pack : (i + 1) * pack, :blk]
            pre_gate = pre_gate + dot(x, wg_v[i * blk : (i + 1) * blk, cols])
            pre_up = pre_up + dot(x, wu_v[i * blk : (i + 1) * blk, cols])
        act[:, cols] = (
            (pre_up + 1.0) * pre_gate * jax.nn.sigmoid(1.702 * pre_gate)
        ).astype(BF16)

    step = 512
    full = ff // step

    def hidden_step(i, carry):
        hidden_cols(pl.ds(pl.multiple_of(i * step, step), step))
        return carry

    lax.fori_loop(0, full, hidden_step, 0)
    if ff % step:
        hidden_cols(pl.ds(full * step, ff - full * step))

    for copy in weights[2]:
        copy.wait()
    chunk = 2 * half
    for k in range(n_cuts):
        low_col, high_col = k * chunk, min((k + 1) * chunk, width)
        yb[:, low_col:high_col] = dot(act[...], wd_v[:, low_col:high_col])
        values = yb[...]
        for i in range(QUARTERS):
            begin = k * blk + i * part
            yq[i * pack : (i + 1) * pack, :part] = values[:, begin : begin + part].astype(BF16)
        blocks = dot(swap, yq[...]).astype(BF16)
        for i in range(n_group):
            se[k, i] = blocks[i * pack : (i + 1) * pack]

        @pl.when(c == k)
        def _(k=k):
            re[me] = se[k, g]

        for dg in range(n_group):
            for ds in range(n_side):
                to_s, to_g = lax.rem(s + ds, n_side), lax.rem(g + dg, n_group)

                def send_rows(k=k, to_s=to_s, to_g=to_g):
                    pltpu.make_async_remote_copy(
                        src_ref=se.at[k, to_g],
                        dst_ref=re.at[me],
                        send_sem=send_e.at[(to_s * n_group + to_g) * n_cuts + k],
                        recv_sem=recv_e.at[me],
                        device_id=at(to_s, to_g, k),
                        device_id_type=MESH,
                    ).start()

                if dg == 0 and ds == 0:
                    pl.when(c != k)(send_rows)
                else:
                    send_rows()

    def other_of(i):
        peer = lax.rem(me + i, total)
        return pltpu.make_async_remote_copy(
            src_ref=se.at[0, 0],
            dst_ref=re.at[peer],
            send_sem=send_e.at[peer],
            recv_sem=recv_e.at[peer],
            device_id=at(
                lax.div(peer, n_group * n_cuts),
                lax.rem(lax.div(peer, n_cuts), n_group),
                lax.rem(peer, n_cuts),
            ),
            device_id_type=MESH,
        )

    def receive(i, carry):
        other_of(i).wait_recv()
        return carry

    lax.fori_loop(1, total, receive, 0)
    returned = re[...].reshape(wide, re.shape[2])
    moe = dot(combine[0], returned) + dot(combine[1], returned)
    moe = jnp.concatenate(
        [moe[i * reqs : (i + 1) * reqs, :part] for i in range(QUARTERS)], axis=1
    )
    out_ref[...] = (mid[pl.ds(pl.multiple_of(c * reqs, reqs), reqs), :] + moe).astype(BF16)

    for copy in sends:
        copy.wait_send()
    for i in range(plane):
        to = lax.rem(d + i, plane)

        def sum_sent(to=to):
            pltpu.make_async_remote_copy(
                src_ref=sc,
                dst_ref=rc.at[g, col_half],
                send_sem=send_c.at[to],
                recv_sem=recv_c.at[g, col_half],
                device_id=at(lax.div(to, n_cuts), row_block, lax.rem(to, n_cuts)),
                device_id_type=MESH,
            ).wait_send()

        if i == 0:
            pl.when(row_block != g)(sum_sent)
        else:
            sum_sent()

    def sent(i, carry):
        other_of(i).wait_send()
        return carry

    lax.fori_loop(1, total, sent, 0)


def up_to(value, by):
    return -(-value // by) * by


def fused_fits(queries, cache_keys, residual_in, expert_gate, adapter_in, router, routes, sinks):
    n_side, n_group, n_cuts = (lax.axis_size(name) for name in ("side", "group", "cuts"))
    reqs, width = residual_in.shape
    blk = width // n_group
    heads = sinks.shape[0]
    return (
        n_group == n_cuts
        and n_side == 2
        and n_group == QUARTERS
        and cache_keys.shape[1] == 1
        and expert_gate.shape[1] == FF
        and router.shape[1] == n_side * n_group * n_cuts
        and width % (n_group * QUARTERS) == 0
        and blk % 16 == 0
        and reqs == 16
        and CAP * n_group == 16
        and heads == 8
        and 3 * width * up_to(FF, 128) * 2 <= 50 * 2**20
    )


def fused(
    queries,
    cache_keys,
    cache_values,
    new_keys,
    new_values,
    lengths,
    head_sinks,
    attn_proj,
    residual_in,
    norm_gain,
    router,
    expert_routes,
    expert_gate,
    expert_up,
    expert_down,
    adapter_in,
    adapter_gate,
    adapter_up,
):
    n_side, n_group, n_cuts = (lax.axis_size(name) for name in ("side", "group", "cuts"))
    reqs, width = residual_in.shape
    ff = expert_gate.shape[1]
    heads, hd, cache = head_sinks.shape[0], cache_keys.shape[2], cache_keys.shape[3]
    blk = width // n_group
    half = up_to(-(-blk // 2), 128)
    experts, topk = router.shape[1], expert_routes.shape[1]
    plane = n_side * n_cuts
    total = plane * n_group
    pack = n_group * CAP
    lanes = up_to(blk // QUARTERS, 128)
    sizes = (n_side, n_group, n_cuts, reqs, heads, hd, width, ff, blk, experts, topk, half)
    squeezed = (reqs, hd, cache)
    gain = norm_gain.reshape(1, width)
    operands = (
        queries,
        new_keys,
        new_values,
        cache_keys.reshape(squeezed),
        cache_values.reshape(squeezed),
        attn_proj,
        residual_in,
        gain,
        router,
        expert_routes,
        expert_gate,
        expert_up,
        expert_down,
        adapter_in,
        adapter_gate,
        adapter_up,
    )
    dma = pltpu.SemaphoreType.DMA
    any_space = pl.BlockSpec(memory_space=pl.ANY)
    smem = pl.BlockSpec(memory_space=pltpu.SMEM)
    scratch = [pltpu.VMEM(x.shape, x.dtype) for x in operands]
    scratch += [
        pltpu.VMEM((n_group, reqs, heads * hd), BF16),
        pltpu.VMEM((n_group * reqs, 2 * half), BF16),
        pltpu.VMEM((plane, reqs, half), BF16),
        pltpu.VMEM((reqs, half), BF16),
        pltpu.VMEM((n_group, 2, reqs, half), BF16),
        pltpu.VMEM((n_group * reqs, 2 * half), BF16),
        pltpu.VMEM((n_group * reqs, blk), F32),
        pltpu.VMEM((n_group, pack, 2 * half), BF16),
        pltpu.VMEM((n_group, pack, 2 * half), BF16),
        pltpu.VMEM((n_group * pack, 2 * half), BF16),
        pltpu.VMEM((pack, ff), BF16),
        pltpu.VMEM((pack, width), F32),
        pltpu.VMEM((QUARTERS * pack, lanes), BF16),
        pltpu.VMEM((n_cuts, n_group, QUARTERS * CAP, lanes), BF16),
        pltpu.VMEM((total, QUARTERS * CAP, lanes), BF16),
        dma((13,)),
        dma((3, n_group)),
        dma((n_group,)),
        dma((n_group,)),
        dma((plane,)),
        dma((plane,)),
        dma((plane,)),
        dma((n_group, 2)),
        dma((n_group,)),
        dma((n_group,)),
        dma((total,)),
        dma((total,)),
    ]
    return pl.pallas_call(
        functools.partial(layer_kernel, sizes),
        out_shape=jax.ShapeDtypeStruct((reqs, blk), BF16),
        in_specs=[smem, smem] + [any_space] * len(operands),
        out_specs=pl.BlockSpec(memory_space=pltpu.VMEM),
        scratch_shapes=scratch,
        compiler_params=pltpu.CompilerParams(
            collective_id=0, has_side_effects=True, vmem_limit_bytes=62 * 2**20
        ),
        cost_estimate=pl.CostEstimate(
            flops=6 * pack * width * ff, bytes_accessed=6 * width * ff, transcendentals=0
        ),
    )(lengths, head_sinks, *operands)


def shards(
    queries,
    cache_keys,
    cache_values,
    new_keys,
    new_values,
    lengths,
    head_sinks,
    attn_proj,
    residual_in,
    norm_gain,
    router,
    expert_routes,
    expert_gate,
    expert_up,
    expert_down,
    adapter_in,
    adapter_gate,
    adapter_up,
):
    if fused_fits(
        queries,
        cache_keys,
        residual_in,
        expert_gate,
        adapter_in,
        router,
        expert_routes,
        head_sinks,
    ):
        return fused(
            queries,
            cache_keys,
            cache_values,
            new_keys,
            new_values,
            lengths,
            head_sinks,
            attn_proj,
            residual_in,
            norm_gain,
            router,
            expert_routes,
            expert_gate,
            expert_up,
            expert_down,
            adapter_in,
            adapter_gate,
            adapter_up,
        )
    n_group = lax.axis_size("group")
    n_cuts = lax.axis_size("cuts")
    side_index = lax.axis_index("side")
    cut_index = lax.axis_index("cuts")
    attn_out = attention_rows(
        queries, cache_keys, cache_values, new_keys, new_values, lengths, head_sinks
    )
    req_count = attn_out.shape[0]
    width = residual_in.shape[1]
    quarter = width // n_cuts
    partial_cols = jnp.dot(
        lax.all_gather(attn_out, "group", axis=0, tiled=True),
        attn_proj,
        preferred_element_type=jnp.float32,
    )
    partial_rows = lax.all_to_all(
        partial_cols.astype(jnp.bfloat16), "group", split_axis=0, concat_axis=1, tiled=True
    ).astype(partial_cols.dtype)
    projected = lax.psum(partial_rows.astype(jnp.bfloat16), ("side", "cuts")).astype(jnp.float32)
    middle = residual_in.astype(jnp.float32) + projected
    inverse = lax.rsqrt(jnp.mean(middle * middle, axis=1, keepdims=True) + epsilon)
    normed = (middle * inverse * norm_gain).astype(jnp.bfloat16)
    logits = jnp.dot(normed, router, preferred_element_type=jnp.float32)
    expert_count = router.shape[1]
    chosen = (
        expert_routes[:, :, None] == lax.broadcasted_iota(jnp.int32, (1, 1, expert_count), 2)
    ).astype(jnp.float32)
    picked = jnp.sum(chosen * logits[:, None, :], axis=2)
    raw_gate = jax.nn.sigmoid(picked)
    gate_weights = raw_gate / jnp.sum(raw_gate, axis=1, keepdims=True)
    member = jnp.sum(chosen, axis=1)
    earlier = (
        lax.broadcasted_iota(jnp.int32, (req_count, req_count), 1)
        < lax.broadcasted_iota(jnp.int32, (req_count, req_count), 0)
    ).astype(jnp.float32)
    before = jnp.sum(earlier[:, :, None] * member[None, :, :], axis=1)
    slot_pos = jnp.sum(chosen * before[:, None, :], axis=2).astype(jnp.int32)
    slice_width = expert_gate.shape[1]
    local_count = max(slice_width // FF, 1)
    hidden_local = min(slice_width, FF)
    rank_width = adapter_in.shape[1]
    dest_groups = lax.broadcasted_iota(jnp.int32, (n_group, 1), 0)
    row_base = (side_index * n_group + dest_groups) * n_cuts
    local_table = (row_base + cut_index) * slice_width // FF + lax.broadcasted_iota(
        jnp.int32, (1, local_count), 1
    )
    ones_weight = jnp.ones(gate_weights.shape, jnp.float32)
    gate_cols = expert_gate.reshape(width, local_count, hidden_local)
    up_cols = expert_up.reshape(width, local_count, hidden_local)
    down_rows = expert_down.reshape(local_count, hidden_local, width)
    adapt_gate = adapter_gate.reshape(rank_width, local_count, hidden_local)
    adapt_up = adapter_up.reshape(rank_width, local_count, hidden_local)
    placement = routing_matrix(local_table, expert_routes, slot_pos, ones_weight).astype(
        jnp.bfloat16
    )
    outgoing = jnp.einsum(
        "gjcr,rd->gjcd", placement, normed, preferred_element_type=jnp.float32
    ).astype(jnp.bfloat16)
    row_block = lax.all_to_all(outgoing, "group", split_axis=0, concat_axis=0, tiled=True)
    pre_gate = jnp.einsum(
        "gjcd,djh->gjch", row_block, gate_cols, preferred_element_type=jnp.float32
    )
    pre_up = jnp.einsum("gjcd,djh->gjch", row_block, up_cols, preferred_element_type=jnp.float32)
    low_code = jnp.einsum(
        "gjcd,dr->gjcr", row_block, adapter_in, preferred_element_type=jnp.float32
    ).astype(jnp.bfloat16)
    finish_pre_gate = pre_gate
    finish_pre_up = pre_up
    finish_pre_gate = finish_pre_gate + jnp.einsum(
        "gjcr,rjh->gjch", low_code, adapt_gate, preferred_element_type=jnp.float32
    )
    finish_pre_up = finish_pre_up + jnp.einsum(
        "gjcr,rjh->gjch", low_code, adapt_up, preferred_element_type=jnp.float32
    )
    activated = (
        (finish_pre_up + 1.0) * finish_pre_gate * jax.nn.sigmoid(1.702 * finish_pre_gate)
    ).astype(jnp.bfloat16)
    partial_value = jnp.einsum(
        "gjch,jhd->gjcd", activated, down_rows, preferred_element_type=jnp.float32
    )
    returned = lax.all_to_all(
        partial_value.astype(jnp.bfloat16), "group", split_axis=0, concat_axis=0, tiled=True
    ).astype(partial_value.dtype)
    weighting = routing_matrix(local_table, expert_routes, slot_pos, gate_weights)
    moe_part = jnp.einsum("gjcr,gjcd->rd", weighting, returned, precision=lax.Precision.HIGHEST)
    moe_cols = lax.psum_scatter(
        moe_part.astype(jnp.bfloat16), "cuts", scatter_dimension=1, tiled=True
    )
    moe_total = lax.psum(moe_cols, "side").astype(jnp.float32)
    middle_cols = lax.dynamic_slice_in_dim(middle, cut_index * quarter, quarter, 1)
    return (middle_cols + moe_total).astype(jnp.bfloat16)


def solution(mesh):
    placed = (
        P("group", ("side", "cuts")),
        P("group", ("side", "cuts"), None, None),
        P("group", ("side", "cuts"), None, None),
        P("group", ("side", "cuts")),
        P("group", ("side", "cuts")),
        P("group"),
        P(("side", "cuts")),
        P(("side", "cuts"), "group"),
        P("group", None),
        P(),
        P(),
        P("group", None),
        P(None, ("side", "group", "cuts")),
        P(None, ("side", "group", "cuts")),
        P(("side", "group", "cuts"), None),
        P(),
        P(None, ("side", "group", "cuts")),
        P(None, ("side", "group", "cuts")),
    )
    return jax.shard_map(
        shards, mesh=mesh, in_specs=placed, out_specs=P("group", "cuts"), check_vma=False
    )
```

```python
import functools
import math

import jax
import jax.numpy as jnp
from jax import lax
from jax.experimental import pallas as pl
from jax.experimental.pallas import tpu as pltpu
from jax.sharding import PartitionSpec as P

FF = 2880
CAP = 4


epsilon = 1e-05


def attention_rows(queries, cache_keys, cache_values, new_keys, new_values, lengths, head_sinks):
    req_count = queries.shape[0]
    kv_count = cache_keys.shape[1]
    head_dim = cache_keys.shape[2]
    cache_len = cache_keys.shape[3]
    head_count = head_sinks.shape[0]
    group_size = head_count // kv_count
    query_rows = queries.reshape(req_count, kv_count, group_size, head_dim)
    fresh_key = new_keys.reshape(req_count, kv_count, head_dim)
    fresh_value = new_values.reshape(req_count, kv_count, head_dim)
    scaling = 1.0 / math.sqrt(head_dim)
    scores = (
        jnp.einsum("rkgd,rkdl->rkgl", query_rows, cache_keys, preferred_element_type=jnp.float32)
        * scaling
    )
    own_score = (
        jnp.einsum("rkgd,rkd->rkg", query_rows, fresh_key, preferred_element_type=jnp.float32)
        * scaling
    )
    validity = (
        lax.broadcasted_iota(jnp.int32, (req_count, 1, 1, cache_len), 3)
        < lengths[:, None, None, None]
    )
    scores = jnp.where(validity, scores, -1e30)
    sink_logit = head_sinks.reshape(1, kv_count, group_size)
    highest = jnp.maximum(jnp.maximum(jnp.max(scores, axis=3), own_score), sink_logit)
    exp_terms = jnp.where(validity, jnp.exp(scores - highest[..., None]), 0.0)
    own_term = jnp.exp(own_score - highest)
    denominator = jnp.sum(exp_terms, axis=3) + own_term + jnp.exp(sink_logit - highest)
    attn_probs = (exp_terms / denominator[..., None]).astype(jnp.bfloat16)
    own_prob = (own_term / denominator).astype(jnp.bfloat16)
    attn_mix = jnp.einsum(
        "rkgl,rkdl->rkgd", attn_probs, cache_values, preferred_element_type=jnp.float32
    )
    attn_mix = (
        attn_mix
        + own_prob.astype(jnp.float32)[..., None] * fresh_value.astype(jnp.float32)[:, :, None, :]
    )
    return attn_mix.astype(jnp.bfloat16).reshape(req_count, head_count * head_dim)


def routing_matrix(expert_table, expert_routes, slot_pos, weights):
    slot_total = CAP
    matched = (expert_routes[None, None, :, :] == expert_table[:, :, None, None]).astype(
        jnp.float32
    )
    slot_hot = (
        slot_pos[:, :, None] == lax.broadcasted_iota(jnp.int32, (1, 1, slot_total), 2)
    ).astype(jnp.float32)
    return jnp.einsum(
        "gjrk,rkc->gjcr",
        matched * weights[None, None, :, :],
        slot_hot,
        precision=lax.Precision.HIGHEST,
    )

MESH = pl.DeviceIdType.MESH
F32 = jnp.float32
BF16 = jnp.bfloat16
QUARTERS = 4


def idiv(value, by):
    if by & (by - 1) == 0:
        return lax.shift_right_logical(value, jnp.full_like(value, by.bit_length() - 1))
    return lax.div(value, jnp.full_like(value, by))


def imod(value, by):
    return value - idiv(value, by) * by


def iota(shape, dim):
    return lax.broadcasted_iota(jnp.int32, shape, dim)


def hot(condition):
    return jnp.where(condition, 1.0, 0.0)


def dot(a, b):
    return jnp.dot(a, b, preferred_element_type=F32)


def dot_nt(a, b):
    return lax.dot_general(a, b, (((1,), (1,)), ((), ())), preferred_element_type=F32)


def swap_digits(outer, inner, tail, dtype):
    size = outer * inner * tail
    row, col = iota((size, size), 0), iota((size, size), 1)
    r_in, r_out, r_tail = idiv(row, outer * tail), imod(idiv(row, tail), outer), imod(row, tail)
    wanted = (r_out * inner + r_in) * tail + r_tail
    return hot(col == wanted).astype(dtype)


def layer_kernel(
    sizes,
    len_ref,
    sink_ref,
    q_hbm,
    nk_hbm,
    nv_hbm,
    ck_hbm,
    cv_hbm,
    proj_hbm,
    resid_hbm,
    gain_hbm,
    router_hbm,
    routes_hbm,
    wg_hbm,
    wu_hbm,
    wd_hbm,
    ain_hbm,
    ag_hbm,
    au_hbm,
    out_ref,
    q_v,
    nk_v,
    nv_v,
    ck_v,
    cv_v,
    proj_v,
    resid_v,
    gain_v,
    router_v,
    routes_v,
    wg_v,
    wu_v,
    wd_v,
    ain_v,
    ag_v,
    au_v,
    agb,
    pb,
    rb,
    sc,
    rc,
    nst,
    rs,
    mid,
    sd,
    xd,
    xp,
    act,
    yb,
    yq,
    se,
    re,
    fs,
    fr,
    in_sem,
    w_sem,
    send_a,
    recv_a,
    send_b,
    recv_b,
    send_c,
    recv_c,
    send_d,
    recv_d,
    send_e,
    recv_e,
    send_f,
    recv_f,
):
    n_side, n_group, n_cuts, reqs, heads, hd, width, ff, blk, experts, topk, half = sizes
    plane = n_side * n_cuts
    total = plane * n_group
    part = blk // QUARTERS
    s = lax.axis_index("side")
    g = lax.axis_index("group")
    c = lax.axis_index("cuts")
    d = s * n_cuts + c
    me = (s * n_group + g) * n_cuts + c
    mine_e = g * n_cuts + c

    def at(side, group, cut):
        return {"side": side, "group": group, "cuts": cut}

    first = [(q_hbm, q_v), (nk_hbm, nk_v), (nv_hbm, nv_v), (ck_hbm, ck_v), (cv_hbm, cv_v)]
    second = [
        (proj_hbm, proj_v),
        (resid_hbm, resid_v),
        (gain_hbm, gain_v),
        (routes_hbm, routes_v),
        (router_hbm, router_v),
        (ain_hbm, ain_v),
        (ag_hbm, ag_v),
        (au_hbm, au_v),
    ]
    small = [
        pltpu.make_async_copy(a, b, in_sem.at[i]) for i, (a, b) in enumerate(first + second)
    ]
    for copy in small:
        copy.start()
    rows = width // n_group
    weights = []
    for m, (a, b) in enumerate(((wg_hbm, wg_v), (wu_hbm, wu_v), (wd_hbm, wd_v))):
        weights.append(
            [
                pltpu.make_async_copy(
                    a.at[pl.ds(i * rows, rows)], b.at[pl.ds(i * rows, rows)], w_sem.at[m, i]
                )
                for i in range(n_group)
            ]
        )

    def fetch(m):
        for copy in weights[m]:
            copy.start()

    barrier = pltpu.get_barrier_semaphore()

    def greet(i, carry):
        other = lax.rem(me + i, total)
        pl.semaphore_signal(
            barrier,
            inc=1,
            device_id=at(
                lax.div(other, n_group * n_cuts),
                lax.rem(lax.div(other, n_cuts), n_group),
                lax.rem(other, n_cuts),
            ),
            device_id_type=MESH,
        )
        return carry

    lax.fori_loop(1, total, greet, 0)

    pb[...] = jnp.zeros_like(pb)
    nst[...] = jnp.zeros_like(nst)
    sc[...] = jnp.zeros_like(sc)
    yq[...] = jnp.zeros_like(yq)

    n_rows = reqs * heads
    for copy in small[:4]:
        copy.wait()
    fetch(0)
    q = q_v[...]
    q_stack = jnp.concatenate([q[:, h * hd : (h + 1) * hd] for h in range(heads)], axis=0)
    q_rows = dot(swap_digits(heads, reqs, 1, BF16), q_stack)
    spread = hot(
        idiv(iota((n_rows, reqs), 0), heads) == iota((n_rows, reqs), 1)
    ).astype(BF16)
    nk_rows = dot(spread, nk_v[...])
    scaling = 1.0 / math.sqrt(hd)
    cache = ck_v.shape[2]
    place = iota((heads, cache), 1)
    scores = []
    for r in range(reqs):
        raw = dot(q_rows[r * heads : (r + 1) * heads].astype(BF16), ck_v[r]) * scaling
        scores.append(jnp.where(place < len_ref[r], raw, -1e30))
    scores = jnp.concatenate(scores, axis=0)
    own = jnp.sum(q_rows * nk_rows, axis=1, keepdims=True) * scaling
    head_of = iota((heads, 1), 0)
    sink = jnp.zeros((heads, 1), F32)
    for h in range(heads):
        sink = jnp.where(head_of == h, sink_ref[h], sink)
    sink = jnp.concatenate([sink] * reqs, axis=0)
    top = jnp.maximum(jnp.maximum(jnp.max(scores, axis=1, keepdims=True), own), sink)
    terms = jnp.exp(scores - top)
    own_term = jnp.exp(own - top)
    denominator = jnp.sum(terms, axis=1, keepdims=True) + own_term + jnp.exp(sink - top)
    probs = terms / denominator
    own_prob = (own_term / denominator).astype(BF16).astype(F32)
    small[4].wait()
    nv_rows = dot(spread, nv_v[...])
    mixed = jnp.concatenate(
        [
            dot_nt(probs[r * heads : (r + 1) * heads].astype(BF16), cv_v[r])
            for r in range(reqs)
        ],
        axis=0,
    )
    mixed = (mixed + own_prob * nv_rows).astype(BF16)
    mixed = dot(swap_digits(reqs, heads, 1, BF16), mixed)
    agb[g] = jnp.concatenate(
        [mixed[h * reqs : (h + 1) * reqs] for h in range(heads)], axis=1
    ).astype(BF16)

    pl.semaphore_wait(barrier, total - 1)

    sends = []
    for i in range(1, n_group):
        to = lax.rem(g + i, n_group)
        copy = pltpu.make_async_remote_copy(
            src_ref=agb.at[g],
            dst_ref=agb.at[g],
            send_sem=send_a.at[to],
            recv_sem=recv_a.at[g],
            device_id=at(s, to, c),
            device_id_type=MESH,
        )
        copy.start()
        sends.append(copy)

    for copy in small[5:]:
        copy.wait()
    eye = hot(iota((reqs, reqs), 0) == iota((reqs, reqs), 1)).astype(BF16)
    routes = dot_nt(eye, routes_v[...].astype(F32).astype(BF16))
    lane_e = iota((reqs, experts), 1).astype(F32)
    chosen = [hot(routes[:, j : j + 1] == lane_e) for j in range(topk)]
    member = functools.reduce(jnp.add, chosen)
    earlier = hot(iota((reqs, reqs), 1) < iota((reqs, reqs), 0)).astype(BF16)
    before = dot(earlier, member.astype(BF16))
    n_pack = n_group * n_group * CAP
    row_e = iota((n_pack, experts), 0)
    dest = (s * n_group + idiv(row_e, n_group * CAP)) * n_cuts + c
    picks = hot(iota((n_pack, experts), 1) == dest).astype(BF16)
    is_member = dot_nt(picks, member.astype(BF16))
    is_before = dot_nt(picks, before.astype(BF16))
    slot_of = imod(iota((n_pack, reqs), 0), CAP).astype(F32)
    placed = is_member * hot(is_before == slot_of)
    n_stack = n_group * reqs
    tile_out = hot(
        imod(iota((reqs, n_stack), 1), reqs) == iota((reqs, n_stack), 0)
    ).astype(BF16)
    place_rows = dot(placed.astype(BF16), tile_out)
    same_blk = imod(idiv(iota((n_pack, n_stack), 0), CAP), n_group) == idiv(
        iota((n_pack, n_stack), 1), reqs
    )
    place_rows = jnp.where(same_blk, place_rows, 0.0).astype(BF16)
    resid = resid_v[...]
    router_t, ain_t = router_v[...], ain_v[...]
    for i in range(n_group):
        rs[i, :experts] = router_t[:, i * blk : (i + 1) * blk]
        rs[i, experts:] = ain_t[:, i * blk : (i + 1) * blk]

    for i in range(1, n_group):
        peer = lax.rem(g + i, n_group)
        pltpu.make_async_remote_copy(
            src_ref=agb.at[g],
            dst_ref=agb.at[peer],
            send_sem=send_a.at[peer],
            recv_sem=recv_a.at[peer],
            device_id=at(s, peer, c),
            device_id_type=MESH,
        ).wait_recv()
    gathered = jnp.concatenate([agb[i] for i in range(n_group)], axis=0)
    pb[:, :blk] = dot_nt(gathered, proj_v[...]).astype(BF16)

    for i in range(1, plane):
        to = lax.rem(d + i, plane)
        copy = pltpu.make_async_remote_copy(
            src_ref=pb.at[
                pl.ds(pl.multiple_of(lax.div(to, 2) * reqs, reqs), reqs),
                pl.ds(pl.multiple_of(lax.rem(to, 2) * half, half), half),
            ],
            dst_ref=rb.at[d],
            send_sem=send_b.at[to],
            recv_sem=recv_b.at[d],
            device_id=at(lax.div(to, n_cuts), g, lax.rem(to, n_cuts)),
            device_id_type=MESH,
        )
        copy.start()
        sends.append(copy)
    fetch(1)
    row_block, col_half = lax.div(d, 2), lax.rem(d, 2)
    total_block = pb[
        pl.ds(pl.multiple_of(row_block * reqs, reqs), reqs),
        pl.ds(pl.multiple_of(col_half * half, half), half),
    ].astype(F32)
    for i in range(1, plane):
        peer = lax.rem(d + i, plane)
        pltpu.make_async_remote_copy(
            src_ref=sc,
            dst_ref=rb.at[peer],
            send_sem=send_b.at[peer],
            recv_sem=recv_b.at[peer],
            device_id=at(lax.div(peer, n_cuts), g, lax.rem(peer, n_cuts)),
            device_id_type=MESH,
        ).wait_recv()
        total_block = total_block + rb[peer].astype(F32)
    summed = total_block.astype(BF16)
    sc[...] = summed

    for i in range(plane):
        to = lax.rem(d + i, plane)

        def send_sum(to=to):
            pltpu.make_async_remote_copy(
                src_ref=sc,
                dst_ref=rc.at[g, col_half],
                send_sem=send_c.at[to],
                recv_sem=recv_c.at[g, col_half],
                device_id=at(lax.div(to, n_cuts), row_block, lax.rem(to, n_cuts)),
                device_id_type=MESH,
            ).start()

        if i == 0:
            pl.when(row_block != g)(send_sum)

            @pl.when(row_block == g)
            def _():
                rc[g, col_half] = summed
        else:
            send_sum()

    fetch(2)

    def sums_from(i, h):
        pos = 2 * g + h
        return pltpu.make_async_remote_copy(
            src_ref=sc,
            dst_ref=rc.at[i, h],
            send_sem=send_c.at[0],
            recv_sem=recv_c.at[i, h],
            device_id=at(lax.div(pos, n_cuts), i, lax.rem(pos, n_cuts)),
            device_id_type=MESH,
        )

    squares = jnp.zeros((reqs, 1), F32)
    for i in range(n_group):
        for h in range(2):
            mine = jnp.logical_and(i == g, 2 * g + h == d)

            @pl.when(jnp.logical_not(mine))
            def _(i=i, h=h):
                sums_from(i, h).wait_recv()

    middles = []
    for i in range(n_group):
        projected = jnp.concatenate([rc[i, 0], rc[i, 1]], axis=1)[:, :blk].astype(F32)
        middle = resid[:, i * blk : (i + 1) * blk].astype(F32) + projected
        mid[i * reqs : (i + 1) * reqs, :] = middle
        squares = squares + jnp.sum(middle * middle, axis=1, keepdims=True)
        middles.append(middle)
    inverse = lax.rsqrt(squares / width + epsilon)
    gain = gain_v[...].reshape(1, width)
    for i in range(n_group):
        normed = (middles[i] * inverse * gain[:, i * blk : (i + 1) * blk]).astype(BF16)
        nst[i * reqs : (i + 1) * reqs, :blk] = normed

    packed = dot(place_rows, nst[...]).astype(BF16)
    pack = n_group * CAP
    for i in range(n_group):
        sd[i] = packed[i * pack : (i + 1) * pack]
    for i in range(1, n_group):
        to = lax.rem(g + i, n_group)
        copy = pltpu.make_async_remote_copy(
            src_ref=sd.at[to],
            dst_ref=xd.at[g],
            send_sem=send_d.at[to],
            recv_sem=recv_d.at[g],
            device_id=at(s, to, c),
            device_id_type=MESH,
        )
        copy.start()
        sends.append(copy)
    xd[g] = sd[g]

    logits = jnp.zeros((reqs, experts), F32)
    for i in range(n_group):
        logits = logits + dot_nt(nst[i * reqs : (i + 1) * reqs, :blk], rs[i, :experts])
    raw = [jax.nn.sigmoid(jnp.sum(hits * logits, axis=1, keepdims=True)) for hits in chosen]
    raw_sum = functools.reduce(jnp.add, raw)
    weight = functools.reduce(jnp.add, [hits * (x / raw_sum) for hits, x in zip(chosen, raw)])
    weight_hi = weight.astype(BF16)
    weight_lo = (weight - weight_hi.astype(F32)).astype(BF16)
    unit = QUARTERS * CAP
    flank = n_group * n_cuts
    wide = flank * unit
    widen = hot(
        s * flank + idiv(iota((experts, wide), 1), unit) == iota((experts, wide), 0)
    ).astype(BF16)
    slot_ok = dot(before.astype(BF16), widen) == imod(iota((reqs, wide), 1), CAP).astype(F32)
    quarter_of = imod(idiv(iota((reqs, wide), 1), CAP), QUARTERS)
    combine = []
    for value in (weight_hi, weight_lo):
        spread_w = jnp.where(slot_ok, dot(value, widen), 0.0)
        combine.append(
            jnp.concatenate(
                [jnp.where(quarter_of == i, spread_w, 0.0) for i in range(QUARTERS)], axis=0
            ).astype(BF16)
        )

    for i in range(1, n_group):
        peer = lax.rem(g + i, n_group)
        pltpu.make_async_remote_copy(
            src_ref=sd.at[peer],
            dst_ref=xd.at[peer],
            send_sem=send_d.at[peer],
            recv_sem=recv_d.at[peer],
            device_id=at(s, peer, c),
            device_id_type=MESH,
        ).wait_recv()
    arrived = jnp.concatenate([xd[i] for i in range(n_group)], axis=0)
    swap = swap_digits(n_group, n_group, CAP, BF16)
    xp[...] = dot(swap, arrived).astype(BF16)

    low = jnp.zeros((pack, ain_v.shape[0]), F32)
    for i in range(n_group):
        low = low + dot_nt(xp[i * pack : (i + 1) * pack, :blk], rs[i, experts:])
    low = low.astype(BF16)

    for copies in weights[:2]:
        for copy in copies:
            copy.wait()

    def hidden_cols(cols):
        pre_gate = dot(low, ag_v[:, cols])
        pre_up = dot(low, au_v[:, cols])
        for i in range(n_group):
            x = xp[i * pack : (i + 1) * pack, :blk]
            pre_gate = pre_gate + dot(x, wg_v[i * blk : (i + 1) * blk, cols])
            pre_up = pre_up + dot(x, wu_v[i * blk : (i + 1) * blk, cols])
        act[:, cols] = (
            (pre_up + 1.0) * pre_gate * jax.nn.sigmoid(1.702 * pre_gate)
        ).astype(BF16)

    step = 512
    full = ff // step

    def hidden_step(i, carry):
        hidden_cols(pl.ds(pl.multiple_of(i * step, step), step))
        return carry

    lax.fori_loop(0, full, hidden_step, 0)
    if ff % step:
        hidden_cols(pl.ds(full * step, ff - full * step))

    for copy in weights[2]:
        copy.wait()
    chunk = 2 * half
    for k in range(n_cuts):
        low_col, high_col = k * chunk, min((k + 1) * chunk, width)
        yb[:, low_col:high_col] = dot(act[...], wd_v[:, low_col:high_col])
        values = yb[...]
        for i in range(QUARTERS):
            begin = k * blk + i * part
            yq[i * pack : (i + 1) * pack, :part] = values[:, begin : begin + part].astype(BF16)
        blocks = dot(swap, yq[...]).astype(BF16)
        for i in range(n_group):
            se[k, i] = blocks[i * pack : (i + 1) * pack]

        @pl.when(c == k)
        def _(k=k):
            re[mine_e] = se[k, g]

        for dg in range(n_group):
            to_g = lax.rem(g + dg, n_group)

            def send_rows(k=k, to_g=to_g):
                pltpu.make_async_remote_copy(
                    src_ref=se.at[k, to_g],
                    dst_ref=re.at[mine_e],
                    send_sem=send_e.at[to_g * n_cuts + k],
                    recv_sem=recv_e.at[mine_e],
                    device_id=at(s, to_g, k),
                    device_id_type=MESH,
                ).start()

            if dg == 0:
                pl.when(c != k)(send_rows)
            else:
                send_rows()

    def other_of(i):
        peer = lax.rem(mine_e + i, flank)
        return pltpu.make_async_remote_copy(
            src_ref=se.at[0, 0],
            dst_ref=re.at[peer],
            send_sem=send_e.at[peer],
            recv_sem=recv_e.at[peer],
            device_id=at(s, lax.div(peer, n_cuts), lax.rem(peer, n_cuts)),
            device_id_type=MESH,
        )

    def receive(i, carry):
        other_of(i).wait_recv()
        return carry

    lax.fori_loop(1, flank, receive, 0)
    returned = re[...].reshape(wide, re.shape[2])
    fs[...] = (dot(combine[0], returned) + dot(combine[1], returned)).astype(BF16)

    across = pltpu.make_async_remote_copy(
        src_ref=fs,
        dst_ref=fr,
        send_sem=send_f.at[0],
        recv_sem=recv_f.at[0],
        device_id=at(1 - s, g, c),
        device_id_type=MESH,
    )
    across.start()
    sends.append(across)
    across.wait_recv()
    moe = fs[...].astype(F32) + fr[...].astype(F32)
    moe = jnp.concatenate(
        [moe[i * reqs : (i + 1) * reqs, :part] for i in range(QUARTERS)], axis=1
    )
    out_ref[...] = (mid[pl.ds(pl.multiple_of(c * reqs, reqs), reqs), :] + moe).astype(BF16)

    for copy in sends:
        copy.wait_send()
    for i in range(plane):
        to = lax.rem(d + i, plane)

        def sum_sent(to=to):
            pltpu.make_async_remote_copy(
                src_ref=sc,
                dst_ref=rc.at[g, col_half],
                send_sem=send_c.at[to],
                recv_sem=recv_c.at[g, col_half],
                device_id=at(lax.div(to, n_cuts), row_block, lax.rem(to, n_cuts)),
                device_id_type=MESH,
            ).wait_send()

        if i == 0:
            pl.when(row_block != g)(sum_sent)
        else:
            sum_sent()

    def sent(i, carry):
        other_of(i).wait_send()
        return carry

    lax.fori_loop(1, flank, sent, 0)


def up_to(value, by):
    return -(-value // by) * by


def fused_fits(queries, cache_keys, residual_in, expert_gate, adapter_in, router, routes, sinks):
    n_side, n_group, n_cuts = (lax.axis_size(name) for name in ("side", "group", "cuts"))
    reqs, width = residual_in.shape
    blk = width // n_group
    heads = sinks.shape[0]
    return (
        n_group == n_cuts
        and n_side == 2
        and n_group == QUARTERS
        and cache_keys.shape[1] == 1
        and expert_gate.shape[1] == FF
        and router.shape[1] == n_side * n_group * n_cuts
        and width % (n_group * QUARTERS) == 0
        and blk % 16 == 0
        and reqs == 16
        and CAP * n_group == 16
        and heads == 8
        and 3 * width * up_to(FF, 128) * 2 <= 50 * 2**20
    )


def fused(
    queries,
    cache_keys,
    cache_values,
    new_keys,
    new_values,
    lengths,
    head_sinks,
    attn_proj,
    residual_in,
    norm_gain,
    router,
    expert_routes,
    expert_gate,
    expert_up,
    expert_down,
    adapter_in,
    adapter_gate,
    adapter_up,
):
    n_side, n_group, n_cuts = (lax.axis_size(name) for name in ("side", "group", "cuts"))
    reqs, width = residual_in.shape
    ff = expert_gate.shape[1]
    heads, hd, cache = head_sinks.shape[0], cache_keys.shape[2], cache_keys.shape[3]
    blk = width // n_group
    half = up_to(-(-blk // 2), 128)
    experts, topk = router.shape[1], expert_routes.shape[1]
    plane = n_side * n_cuts
    pack = n_group * CAP
    lanes = up_to(blk // QUARTERS, 128)
    sizes = (n_side, n_group, n_cuts, reqs, heads, hd, width, ff, blk, experts, topk, half)
    squeezed = (reqs, hd, cache)
    operands = (
        queries,
        new_keys,
        new_values,
        cache_keys.reshape(squeezed),
        cache_values.reshape(squeezed),
        attn_proj.T,
        residual_in,
        norm_gain,
        router.T,
        expert_routes.T,
        expert_gate,
        expert_up,
        expert_down,
        adapter_in.T,
        adapter_gate,
        adapter_up,
    )
    dma = pltpu.SemaphoreType.DMA
    any_space = pl.BlockSpec(memory_space=pl.ANY)
    smem = pl.BlockSpec(memory_space=pltpu.SMEM)
    scratch = [pltpu.VMEM(x.shape, x.dtype) for x in operands]
    scratch += [
        pltpu.VMEM((n_group, reqs, heads * hd), BF16),
        pltpu.VMEM((n_group * reqs, 2 * half), BF16),
        pltpu.VMEM((plane, reqs, half), BF16),
        pltpu.VMEM((reqs, half), BF16),
        pltpu.VMEM((n_group, 2, reqs, half), BF16),
        pltpu.VMEM((n_group * reqs, 2 * half), BF16),
        pltpu.VMEM((n_group, experts + adapter_in.shape[1], blk), BF16),
        pltpu.VMEM((n_group * reqs, blk), F32),
        pltpu.VMEM((n_group, pack, 2 * half), BF16),
        pltpu.VMEM((n_group, pack, 2 * half), BF16),
        pltpu.VMEM((n_group * pack, 2 * half), BF16),
        pltpu.VMEM((pack, ff), BF16),
        pltpu.VMEM((pack, width), F32),
        pltpu.VMEM((QUARTERS * pack, lanes), BF16),
        pltpu.VMEM((n_cuts, n_group, QUARTERS * CAP, lanes), BF16),
        pltpu.VMEM((n_group * n_cuts, QUARTERS * CAP, lanes), BF16),
        pltpu.VMEM((QUARTERS * reqs, lanes), BF16),
        pltpu.VMEM((QUARTERS * reqs, lanes), BF16),
        dma((13,)),
        dma((3, n_group)),
        dma((n_group,)),
        dma((n_group,)),
        dma((plane,)),
        dma((plane,)),
        dma((plane,)),
        dma((n_group, 2)),
        dma((n_group,)),
        dma((n_group,)),
        dma((n_group * n_cuts,)),
        dma((n_group * n_cuts,)),
        dma((1,)),
        dma((1,)),
    ]
    return pl.pallas_call(
        functools.partial(layer_kernel, sizes),
        out_shape=jax.ShapeDtypeStruct((reqs, blk), BF16),
        in_specs=[smem, smem] + [any_space] * len(operands),
        out_specs=pl.BlockSpec(memory_space=pltpu.VMEM),
        scratch_shapes=scratch,
        compiler_params=pltpu.CompilerParams(
            collective_id=0, has_side_effects=True, vmem_limit_bytes=62 * 2**20
        ),
        cost_estimate=pl.CostEstimate(
            flops=6 * pack * width * ff, bytes_accessed=6 * width * ff, transcendentals=0
        ),
    )(lengths, head_sinks, *operands)


def shards(
    queries,
    cache_keys,
    cache_values,
    new_keys,
    new_values,
    lengths,
    head_sinks,
    attn_proj,
    residual_in,
    norm_gain,
    router,
    expert_routes,
    expert_gate,
    expert_up,
    expert_down,
    adapter_in,
    adapter_gate,
    adapter_up,
):
    if fused_fits(
        queries,
        cache_keys,
        residual_in,
        expert_gate,
        adapter_in,
        router,
        expert_routes,
        head_sinks,
    ):
        return fused(
            queries,
            cache_keys,
            cache_values,
            new_keys,
            new_values,
            lengths,
            head_sinks,
            attn_proj,
            residual_in,
            norm_gain,
            router,
            expert_routes,
            expert_gate,
            expert_up,
            expert_down,
            adapter_in,
            adapter_gate,
            adapter_up,
        )
    n_group = lax.axis_size("group")
    n_cuts = lax.axis_size("cuts")
    side_index = lax.axis_index("side")
    cut_index = lax.axis_index("cuts")
    attn_out = attention_rows(
        queries, cache_keys, cache_values, new_keys, new_values, lengths, head_sinks
    )
    req_count = attn_out.shape[0]
    width = residual_in.shape[1]
    quarter = width // n_cuts
    partial_cols = jnp.dot(
        lax.all_gather(attn_out, "group", axis=0, tiled=True),
        attn_proj,
        preferred_element_type=jnp.float32,
    )
    partial_rows = lax.all_to_all(
        partial_cols.astype(jnp.bfloat16), "group", split_axis=0, concat_axis=1, tiled=True
    ).astype(partial_cols.dtype)
    projected = lax.psum(partial_rows.astype(jnp.bfloat16), ("side", "cuts")).astype(jnp.float32)
    middle = residual_in.astype(jnp.float32) + projected
    inverse = lax.rsqrt(jnp.mean(middle * middle, axis=1, keepdims=True) + epsilon)
    normed = (middle * inverse * norm_gain).astype(jnp.bfloat16)
    logits = jnp.dot(normed, router, preferred_element_type=jnp.float32)
    expert_count = router.shape[1]
    chosen = (
        expert_routes[:, :, None] == lax.broadcasted_iota(jnp.int32, (1, 1, expert_count), 2)
    ).astype(jnp.float32)
    picked = jnp.sum(chosen * logits[:, None, :], axis=2)
    raw_gate = jax.nn.sigmoid(picked)
    gate_weights = raw_gate / jnp.sum(raw_gate, axis=1, keepdims=True)
    member = jnp.sum(chosen, axis=1)
    earlier = (
        lax.broadcasted_iota(jnp.int32, (req_count, req_count), 1)
        < lax.broadcasted_iota(jnp.int32, (req_count, req_count), 0)
    ).astype(jnp.float32)
    before = jnp.sum(earlier[:, :, None] * member[None, :, :], axis=1)
    slot_pos = jnp.sum(chosen * before[:, None, :], axis=2).astype(jnp.int32)
    slice_width = expert_gate.shape[1]
    local_count = max(slice_width // FF, 1)
    hidden_local = min(slice_width, FF)
    rank_width = adapter_in.shape[1]
    dest_groups = lax.broadcasted_iota(jnp.int32, (n_group, 1), 0)
    row_base = (side_index * n_group + dest_groups) * n_cuts
    local_table = (row_base + cut_index) * slice_width // FF + lax.broadcasted_iota(
        jnp.int32, (1, local_count), 1
    )
    ones_weight = jnp.ones(gate_weights.shape, jnp.float32)
    gate_cols = expert_gate.reshape(width, local_count, hidden_local)
    up_cols = expert_up.reshape(width, local_count, hidden_local)
    down_rows = expert_down.reshape(local_count, hidden_local, width)
    adapt_gate = adapter_gate.reshape(rank_width, local_count, hidden_local)
    adapt_up = adapter_up.reshape(rank_width, local_count, hidden_local)
    placement = routing_matrix(local_table, expert_routes, slot_pos, ones_weight).astype(
        jnp.bfloat16
    )
    outgoing = jnp.einsum(
        "gjcr,rd->gjcd", placement, normed, preferred_element_type=jnp.float32
    ).astype(jnp.bfloat16)
    row_block = lax.all_to_all(outgoing, "group", split_axis=0, concat_axis=0, tiled=True)
    pre_gate = jnp.einsum(
        "gjcd,djh->gjch", row_block, gate_cols, preferred_element_type=jnp.float32
    )
    pre_up = jnp.einsum("gjcd,djh->gjch", row_block, up_cols, preferred_element_type=jnp.float32)
    low_code = jnp.einsum(
        "gjcd,dr->gjcr", row_block, adapter_in, preferred_element_type=jnp.float32
    ).astype(jnp.bfloat16)
    finish_pre_gate = pre_gate
    finish_pre_up = pre_up
    finish_pre_gate = finish_pre_gate + jnp.einsum(
        "gjcr,rjh->gjch", low_code, adapt_gate, preferred_element_type=jnp.float32
    )
    finish_pre_up = finish_pre_up + jnp.einsum(
        "gjcr,rjh->gjch", low_code, adapt_up, preferred_element_type=jnp.float32
    )
    activated = (
        (finish_pre_up + 1.0) * finish_pre_gate * jax.nn.sigmoid(1.702 * finish_pre_gate)
    ).astype(jnp.bfloat16)
    partial_value = jnp.einsum(
        "gjch,jhd->gjcd", activated, down_rows, preferred_element_type=jnp.float32
    )
    returned = lax.all_to_all(
        partial_value.astype(jnp.bfloat16), "group", split_axis=0, concat_axis=0, tiled=True
    ).astype(partial_value.dtype)
    weighting = routing_matrix(local_table, expert_routes, slot_pos, gate_weights)
    moe_part = jnp.einsum("gjcr,gjcd->rd", weighting, returned, precision=lax.Precision.HIGHEST)
    moe_cols = lax.psum_scatter(
        moe_part.astype(jnp.bfloat16), "cuts", scatter_dimension=1, tiled=True
    )
    moe_total = lax.psum(moe_cols, "side").astype(jnp.float32)
    middle_cols = lax.dynamic_slice_in_dim(middle, cut_index * quarter, quarter, 1)
    return (middle_cols + moe_total).astype(jnp.bfloat16)


def solution(mesh):
    placed = (
        P("group", ("side", "cuts")),
        P("group", ("side", "cuts"), None, None),
        P("group", ("side", "cuts"), None, None),
        P("group", ("side", "cuts")),
        P("group", ("side", "cuts")),
        P("group"),
        P(("side", "cuts")),
        P(("side", "cuts"), "group"),
        P("group", None),
        P(),
        P(),
        P("group", None),
        P(None, ("side", "group", "cuts")),
        P(None, ("side", "group", "cuts")),
        P(("side", "group", "cuts"), None),
        P(),
        P(None, ("side", "group", "cuts")),
        P(None, ("side", "group", "cuts")),
    )
    return jax.shard_map(
        shards, mesh=mesh, in_specs=placed, out_specs=P("group", "cuts"), check_vma=False
    )
```

```python
import functools
import math

import jax
import jax.numpy as jnp
from jax import lax
from jax.experimental import pallas as pl
from jax.experimental.pallas import tpu as pltpu
from jax.sharding import PartitionSpec as P

FF = 2880
CAP = 4


epsilon = 1e-05


def attention_rows(queries, cache_keys, cache_values, new_keys, new_values, lengths, head_sinks):
    req_count = queries.shape[0]
    kv_count = cache_keys.shape[1]
    head_dim = cache_keys.shape[2]
    cache_len = cache_keys.shape[3]
    head_count = head_sinks.shape[0]
    group_size = head_count // kv_count
    query_rows = queries.reshape(req_count, kv_count, group_size, head_dim)
    fresh_key = new_keys.reshape(req_count, kv_count, head_dim)
    fresh_value = new_values.reshape(req_count, kv_count, head_dim)
    scaling = 1.0 / math.sqrt(head_dim)
    scores = (
        jnp.einsum("rkgd,rkdl->rkgl", query_rows, cache_keys, preferred_element_type=jnp.float32)
        * scaling
    )
    own_score = (
        jnp.einsum("rkgd,rkd->rkg", query_rows, fresh_key, preferred_element_type=jnp.float32)
        * scaling
    )
    validity = (
        lax.broadcasted_iota(jnp.int32, (req_count, 1, 1, cache_len), 3)
        < lengths[:, None, None, None]
    )
    scores = jnp.where(validity, scores, -1e30)
    sink_logit = head_sinks.reshape(1, kv_count, group_size)
    highest = jnp.maximum(jnp.maximum(jnp.max(scores, axis=3), own_score), sink_logit)
    exp_terms = jnp.where(validity, jnp.exp(scores - highest[..., None]), 0.0)
    own_term = jnp.exp(own_score - highest)
    denominator = jnp.sum(exp_terms, axis=3) + own_term + jnp.exp(sink_logit - highest)
    attn_probs = (exp_terms / denominator[..., None]).astype(jnp.bfloat16)
    own_prob = (own_term / denominator).astype(jnp.bfloat16)
    attn_mix = jnp.einsum(
        "rkgl,rkdl->rkgd", attn_probs, cache_values, preferred_element_type=jnp.float32
    )
    attn_mix = (
        attn_mix
        + own_prob.astype(jnp.float32)[..., None] * fresh_value.astype(jnp.float32)[:, :, None, :]
    )
    return attn_mix.astype(jnp.bfloat16).reshape(req_count, head_count * head_dim)


def routing_matrix(expert_table, expert_routes, slot_pos, weights):
    slot_total = CAP
    matched = (expert_routes[None, None, :, :] == expert_table[:, :, None, None]).astype(
        jnp.float32
    )
    slot_hot = (
        slot_pos[:, :, None] == lax.broadcasted_iota(jnp.int32, (1, 1, slot_total), 2)
    ).astype(jnp.float32)
    return jnp.einsum(
        "gjrk,rkc->gjcr",
        matched * weights[None, None, :, :],
        slot_hot,
        precision=lax.Precision.HIGHEST,
    )

MESH = pl.DeviceIdType.MESH
F32 = jnp.float32
BF16 = jnp.bfloat16
QUARTERS = 4


def idiv(value, by):
    if by & (by - 1) == 0:
        return lax.shift_right_logical(value, jnp.full_like(value, by.bit_length() - 1))
    return lax.div(value, jnp.full_like(value, by))


def imod(value, by):
    return value - idiv(value, by) * by


def iota(shape, dim):
    return lax.broadcasted_iota(jnp.int32, shape, dim)


def hot(condition):
    return jnp.where(condition, 1.0, 0.0)


def dot(a, b):
    return jnp.dot(a, b, preferred_element_type=F32)


def dot_nt(a, b):
    return lax.dot_general(a, b, (((1,), (1,)), ((), ())), preferred_element_type=F32)


def swap_digits(outer, inner, tail, dtype):
    size = outer * inner * tail
    row, col = iota((size, size), 0), iota((size, size), 1)
    r_in, r_out, r_tail = idiv(row, outer * tail), imod(idiv(row, tail), outer), imod(row, tail)
    wanted = (r_out * inner + r_in) * tail + r_tail
    return hot(col == wanted).astype(dtype)


def layer_kernel(
    sizes,
    len_ref,
    sink_ref,
    q_hbm,
    nk_hbm,
    nv_hbm,
    ck_hbm,
    cv_hbm,
    proj_hbm,
    resid_hbm,
    gain_hbm,
    router_hbm,
    routes_hbm,
    wg_hbm,
    wu_hbm,
    wd_hbm,
    ain_hbm,
    ag_hbm,
    au_hbm,
    out_ref,
    q_v,
    nk_v,
    nv_v,
    ck_v,
    cv_v,
    proj_v,
    resid_v,
    gain_v,
    router_v,
    routes_v,
    wg_v,
    wu_v,
    wd_v,
    ain_v,
    ag_v,
    au_v,
    agb,
    pb,
    rb,
    sc,
    rc,
    nst,
    rs,
    mid,
    sd,
    xd,
    xp,
    pre,
    act,
    yb,
    yq,
    se,
    re,
    fs,
    fr,
    in_sem,
    w_sem,
    send_a,
    recv_a,
    send_b,
    recv_b,
    send_c,
    recv_c,
    send_d,
    recv_d,
    send_e,
    recv_e,
    send_f,
    recv_f,
):
    n_side, n_group, n_cuts, reqs, heads, hd, width, ff, blk, experts, topk, half = sizes
    plane = n_side * n_cuts
    total = plane * n_group
    part = blk // QUARTERS
    s = lax.axis_index("side")
    g = lax.axis_index("group")
    c = lax.axis_index("cuts")
    d = s * n_cuts + c
    me = (s * n_group + g) * n_cuts + c
    mine_e = g * n_cuts + c

    def at(side, group, cut):
        return {"side": side, "group": group, "cuts": cut}

    first = [(q_hbm, q_v), (nk_hbm, nk_v), (nv_hbm, nv_v), (ck_hbm, ck_v), (cv_hbm, cv_v)]
    second = [
        (proj_hbm, proj_v),
        (resid_hbm, resid_v),
        (gain_hbm, gain_v),
        (routes_hbm, routes_v),
        (router_hbm, router_v),
        (ain_hbm, ain_v),
        (ag_hbm, ag_v),
        (au_hbm, au_v),
    ]
    small = [
        pltpu.make_async_copy(a, b, in_sem.at[i]) for i, (a, b) in enumerate(first + second)
    ]
    for copy in small:
        copy.start()
    rows = width // n_group
    weights = []
    for m, (a, b) in enumerate(((wg_hbm, wg_v), (wu_hbm, wu_v), (wd_hbm, wd_v))):
        weights.append(
            [
                pltpu.make_async_copy(
                    a.at[pl.ds(i * rows, rows)], b.at[pl.ds(i * rows, rows)], w_sem.at[m, i]
                )
                for i in range(n_group)
            ]
        )

    def fetch(m, blocks):
        for i in blocks:
            weights[m][i].start()

    early, late = range(n_group // 2), range(n_group // 2, n_group)

    barrier = pltpu.get_barrier_semaphore()

    def greet(i, carry):
        other = lax.rem(me + i, total)
        pl.semaphore_signal(
            barrier,
            inc=1,
            device_id=at(
                lax.div(other, n_group * n_cuts),
                lax.rem(lax.div(other, n_cuts), n_group),
                lax.rem(other, n_cuts),
            ),
            device_id_type=MESH,
        )
        return carry

    lax.fori_loop(1, total, greet, 0)

    pb[...] = jnp.zeros_like(pb)
    nst[...] = jnp.zeros_like(nst)
    sc[...] = jnp.zeros_like(sc)
    yq[...] = jnp.zeros_like(yq)

    n_rows = reqs * heads
    for copy in small[:4]:
        copy.wait()
    fetch(0, range(n_group))
    q = q_v[...]
    q_stack = jnp.concatenate([q[:, h * hd : (h + 1) * hd] for h in range(heads)], axis=0)
    q_rows = dot(swap_digits(heads, reqs, 1, BF16), q_stack)
    spread = hot(
        idiv(iota((n_rows, reqs), 0), heads) == iota((n_rows, reqs), 1)
    ).astype(BF16)
    nk_rows = dot(spread, nk_v[...])
    scaling = 1.0 / math.sqrt(hd)
    cache = ck_v.shape[2]
    place = iota((heads, cache), 1)
    scores = []
    for r in range(reqs):
        raw = dot(q_rows[r * heads : (r + 1) * heads].astype(BF16), ck_v[r]) * scaling
        scores.append(jnp.where(place < len_ref[r], raw, -1e30))
    scores = jnp.concatenate(scores, axis=0)
    own = jnp.sum(q_rows * nk_rows, axis=1, keepdims=True) * scaling
    head_of = iota((heads, 1), 0)
    sink = jnp.zeros((heads, 1), F32)
    for h in range(heads):
        sink = jnp.where(head_of == h, sink_ref[h], sink)
    sink = jnp.concatenate([sink] * reqs, axis=0)
    top = jnp.maximum(jnp.maximum(jnp.max(scores, axis=1, keepdims=True), own), sink)
    terms = jnp.exp(scores - top)
    own_term = jnp.exp(own - top)
    denominator = jnp.sum(terms, axis=1, keepdims=True) + own_term + jnp.exp(sink - top)
    probs = terms / denominator
    own_prob = (own_term / denominator).astype(BF16).astype(F32)
    small[4].wait()
    nv_rows = dot(spread, nv_v[...])
    mixed = jnp.concatenate(
        [
            dot_nt(probs[r * heads : (r + 1) * heads].astype(BF16), cv_v[r])
            for r in range(reqs)
        ],
        axis=0,
    )
    mixed = (mixed + own_prob * nv_rows).astype(BF16)
    mixed = dot(swap_digits(reqs, heads, 1, BF16), mixed)
    agb[g] = jnp.concatenate(
        [mixed[h * reqs : (h + 1) * reqs] for h in range(heads)], axis=1
    ).astype(BF16)

    pl.semaphore_wait(barrier, total - 1)

    sends = []
    for i in range(1, n_group):
        to = lax.rem(g + i, n_group)
        copy = pltpu.make_async_remote_copy(
            src_ref=agb.at[g],
            dst_ref=agb.at[g],
            send_sem=send_a.at[to],
            recv_sem=recv_a.at[g],
            device_id=at(s, to, c),
            device_id_type=MESH,
        )
        copy.start()
        sends.append(copy)

    fetch(1, early)

    for copy in small[5:]:
        copy.wait()
    eye = hot(iota((reqs, reqs), 0) == iota((reqs, reqs), 1)).astype(BF16)
    routes = dot_nt(eye, routes_v[...].astype(F32).astype(BF16))
    lane_e = iota((reqs, experts), 1).astype(F32)
    chosen = [hot(routes[:, j : j + 1] == lane_e) for j in range(topk)]
    member = functools.reduce(jnp.add, chosen)
    earlier = hot(iota((reqs, reqs), 1) < iota((reqs, reqs), 0)).astype(BF16)
    before = dot(earlier, member.astype(BF16))
    n_pack = n_group * n_group * CAP
    row_e = iota((n_pack, experts), 0)
    dest = (s * n_group + idiv(row_e, n_group * CAP)) * n_cuts + c
    picks = hot(iota((n_pack, experts), 1) == dest).astype(BF16)
    is_member = dot_nt(picks, member.astype(BF16))
    is_before = dot_nt(picks, before.astype(BF16))
    slot_of = imod(iota((n_pack, reqs), 0), CAP).astype(F32)
    placed = is_member * hot(is_before == slot_of)
    n_stack = n_group * reqs
    tile_out = hot(
        imod(iota((reqs, n_stack), 1), reqs) == iota((reqs, n_stack), 0)
    ).astype(BF16)
    place_rows = dot(placed.astype(BF16), tile_out)
    same_blk = imod(idiv(iota((n_pack, n_stack), 0), CAP), n_group) == idiv(
        iota((n_pack, n_stack), 1), reqs
    )
    place_rows = jnp.where(same_blk, place_rows, 0.0).astype(BF16)
    resid = resid_v[...]

    for i in range(1, n_group):
        peer = lax.rem(g + i, n_group)
        pltpu.make_async_remote_copy(
            src_ref=agb.at[g],
            dst_ref=agb.at[peer],
            send_sem=send_a.at[peer],
            recv_sem=recv_a.at[peer],
            device_id=at(s, peer, c),
            device_id_type=MESH,
        ).wait_recv()
    gathered = jnp.concatenate([agb[i] for i in range(n_group)], axis=0)
    pb[:, :blk] = dot_nt(gathered, proj_v[...]).astype(BF16)

    for i in range(1, plane):
        to = lax.rem(d + i, plane)
        copy = pltpu.make_async_remote_copy(
            src_ref=pb.at[
                pl.ds(pl.multiple_of(lax.div(to, 2) * reqs, reqs), reqs),
                pl.ds(pl.multiple_of(lax.rem(to, 2) * half, half), half),
            ],
            dst_ref=rb.at[d],
            send_sem=send_b.at[to],
            recv_sem=recv_b.at[d],
            device_id=at(lax.div(to, n_cuts), g, lax.rem(to, n_cuts)),
            device_id_type=MESH,
        )
        copy.start()
        sends.append(copy)
    fetch(1, late)
    row_block, col_half = lax.div(d, 2), lax.rem(d, 2)
    total_block = pb[
        pl.ds(pl.multiple_of(row_block * reqs, reqs), reqs),
        pl.ds(pl.multiple_of(col_half * half, half), half),
    ].astype(F32)
    for i in range(1, plane):
        peer = lax.rem(d + i, plane)
        pltpu.make_async_remote_copy(
            src_ref=sc,
            dst_ref=rb.at[peer],
            send_sem=send_b.at[peer],
            recv_sem=recv_b.at[peer],
            device_id=at(lax.div(peer, n_cuts), g, lax.rem(peer, n_cuts)),
            device_id_type=MESH,
        ).wait_recv()
        total_block = total_block + rb[peer].astype(F32)
    summed = total_block.astype(BF16)
    sc[...] = summed

    for i in range(plane):
        to = lax.rem(d + i, plane)

        def send_sum(to=to):
            pltpu.make_async_remote_copy(
                src_ref=sc,
                dst_ref=rc.at[g, col_half],
                send_sem=send_c.at[to],
                recv_sem=recv_c.at[g, col_half],
                device_id=at(lax.div(to, n_cuts), row_block, lax.rem(to, n_cuts)),
                device_id_type=MESH,
            ).start()

        if i == 0:
            pl.when(row_block != g)(send_sum)

            @pl.when(row_block == g)
            def _():
                rc[g, col_half] = summed
        else:
            send_sum()

    fetch(2, early)
    router_t, ain_t = router_v[...], ain_v[...]
    for i in range(n_group):
        rs[i, :experts] = router_t[:, i * blk : (i + 1) * blk]
        rs[i, experts:] = ain_t[:, i * blk : (i + 1) * blk]

    def sums_from(i, h):
        pos = 2 * g + h
        return pltpu.make_async_remote_copy(
            src_ref=sc,
            dst_ref=rc.at[i, h],
            send_sem=send_c.at[0],
            recv_sem=recv_c.at[i, h],
            device_id=at(lax.div(pos, n_cuts), i, lax.rem(pos, n_cuts)),
            device_id_type=MESH,
        )

    squares = jnp.zeros((reqs, 1), F32)
    for i in range(n_group):
        for h in range(2):
            mine = jnp.logical_and(i == g, 2 * g + h == d)

            @pl.when(jnp.logical_not(mine))
            def _(i=i, h=h):
                sums_from(i, h).wait_recv()

    middles = []
    for i in range(n_group):
        projected = jnp.concatenate([rc[i, 0], rc[i, 1]], axis=1)[:, :blk].astype(F32)
        middle = resid[:, i * blk : (i + 1) * blk].astype(F32) + projected
        mid[i * reqs : (i + 1) * reqs, :] = middle
        squares = squares + jnp.sum(middle * middle, axis=1, keepdims=True)
        middles.append(middle)
    inverse = lax.rsqrt(squares / width + epsilon)
    gain = gain_v[...].reshape(1, width)
    for i in range(n_group):
        normed = (middles[i] * inverse * gain[:, i * blk : (i + 1) * blk]).astype(BF16)
        nst[i * reqs : (i + 1) * reqs, :blk] = normed

    packed = dot(place_rows, nst[...]).astype(BF16)
    pack = n_group * CAP
    for i in range(n_group):
        sd[i] = packed[i * pack : (i + 1) * pack]
    for i in range(1, n_group):
        to = lax.rem(g + i, n_group)
        copy = pltpu.make_async_remote_copy(
            src_ref=sd.at[to],
            dst_ref=xd.at[g],
            send_sem=send_d.at[to],
            recv_sem=recv_d.at[g],
            device_id=at(s, to, c),
            device_id_type=MESH,
        )
        copy.start()
        sends.append(copy)
    fetch(2, late)
    xd[g] = sd[g]

    logits = jnp.zeros((reqs, experts), F32)
    for i in range(n_group):
        logits = logits + dot_nt(nst[i * reqs : (i + 1) * reqs, :blk], rs[i, :experts])
    raw = [jax.nn.sigmoid(jnp.sum(hits * logits, axis=1, keepdims=True)) for hits in chosen]
    raw_sum = functools.reduce(jnp.add, raw)
    weight = functools.reduce(jnp.add, [hits * (x / raw_sum) for hits, x in zip(chosen, raw)])
    weight_hi = weight.astype(BF16)
    weight_lo = (weight - weight_hi.astype(F32)).astype(BF16)
    unit = QUARTERS * CAP
    flank = n_group * n_cuts
    wide = flank * unit
    widen = hot(
        s * flank + idiv(iota((experts, wide), 1), unit) == iota((experts, wide), 0)
    ).astype(BF16)
    slot_ok = dot(before.astype(BF16), widen) == imod(iota((reqs, wide), 1), CAP).astype(F32)
    quarter_of = imod(idiv(iota((reqs, wide), 1), CAP), QUARTERS)
    combine = []
    for value in (weight_hi, weight_lo):
        spread_w = jnp.where(slot_ok, dot(value, widen), 0.0)
        combine.append(
            jnp.concatenate(
                [jnp.where(quarter_of == i, spread_w, 0.0) for i in range(QUARTERS)], axis=0
            ).astype(BF16)
        )

    for i in range(1, n_group):
        peer = lax.rem(g + i, n_group)
        pltpu.make_async_remote_copy(
            src_ref=sd.at[peer],
            dst_ref=xd.at[peer],
            send_sem=send_d.at[peer],
            recv_sem=recv_d.at[peer],
            device_id=at(s, peer, c),
            device_id_type=MESH,
        ).wait_recv()
    arrived = jnp.concatenate([xd[i] for i in range(n_group)], axis=0)
    swap = swap_digits(n_group, n_group, CAP, BF16)
    xp[...] = dot(swap, arrived).astype(BF16)

    low = jnp.zeros((pack, ain_v.shape[0]), F32)
    for i in range(n_group):
        low = low + dot_nt(xp[i * pack : (i + 1) * pack, :blk], rs[i, experts:])
    low = low.astype(BF16)

    for copies in weights[:2]:
        for copy in copies:
            copy.wait()

    def hidden_cols(cols):
        pre_gate = dot(low, ag_v[:, cols])
        pre_up = dot(low, au_v[:, cols])
        for i in range(n_group):
            x = xp[i * pack : (i + 1) * pack, :blk]
            pre_gate = pre_gate + dot(x, wg_v[i * blk : (i + 1) * blk, cols])
            pre_up = pre_up + dot(x, wu_v[i * blk : (i + 1) * blk, cols])
        pre[0, :, cols] = pre_gate
        pre[1, :, cols] = pre_up

    step = 512
    full = ff // step

    def hidden_step(i, carry):
        hidden_cols(pl.ds(pl.multiple_of(i * step, step), step))
        return carry

    lax.fori_loop(0, full, hidden_step, 0)
    if ff % step:
        hidden_cols(pl.ds(full * step, ff - full * step))
    pre_gate, pre_up = pre[0], pre[1]
    act[...] = ((pre_up + 1.0) * pre_gate * jax.nn.sigmoid(1.702 * pre_gate)).astype(BF16)

    for copy in weights[2]:
        copy.wait()
    chunk = 2 * half

    def down(k):
        low_col, high_col = k * chunk, min((k + 1) * chunk, width)
        yb[:, low_col:high_col] = dot(act[...], wd_v[:, low_col:high_col])

    down(0)
    for k in range(n_cuts):
        begin = k * blk // 128 * 128
        values = yb[:, begin : min((k + 1) * chunk, width)]
        for i in range(QUARTERS):
            at_col = k * blk + i * part - begin
            yq[i * pack : (i + 1) * pack, :part] = values[:, at_col : at_col + part].astype(BF16)
        if k < n_cuts - 1:
            down(k + 1)
        blocks = dot(swap, yq[...]).astype(BF16)
        for i in range(n_group):
            se[k, i] = blocks[i * pack : (i + 1) * pack]
        for dg in range(n_group):
            to_g = lax.rem(g + dg, n_group)

            def send_rows(k=k, to_g=to_g):
                pltpu.make_async_remote_copy(
                    src_ref=se.at[k, to_g],
                    dst_ref=re.at[mine_e],
                    send_sem=send_e.at[to_g * n_cuts + k],
                    recv_sem=recv_e.at[mine_e],
                    device_id=at(s, to_g, k),
                    device_id_type=MESH,
                ).start()

            if dg == 0:
                pl.when(c != k)(send_rows)
            else:
                send_rows()
    re[mine_e] = se[c, g]

    def other_of(i):
        peer = lax.rem(mine_e + i, flank)
        return pltpu.make_async_remote_copy(
            src_ref=se.at[0, 0],
            dst_ref=re.at[peer],
            send_sem=send_e.at[peer],
            recv_sem=recv_e.at[peer],
            device_id=at(s, lax.div(peer, n_cuts), lax.rem(peer, n_cuts)),
            device_id_type=MESH,
        )

    def receive(i, carry):
        other_of(i).wait_recv()
        return carry

    lax.fori_loop(1, flank, receive, 0)
    returned = re[...].reshape(wide, re.shape[2])
    fs[...] = (dot(combine[0], returned) + dot(combine[1], returned)).astype(BF16)

    across = pltpu.make_async_remote_copy(
        src_ref=fs,
        dst_ref=fr,
        send_sem=send_f.at[0],
        recv_sem=recv_f.at[0],
        device_id=at(1 - s, g, c),
        device_id_type=MESH,
    )
    across.start()
    sends.append(across)
    across.wait_recv()
    moe = fs[...].astype(F32) + fr[...].astype(F32)
    moe = jnp.concatenate(
        [moe[i * reqs : (i + 1) * reqs, :part] for i in range(QUARTERS)], axis=1
    )
    out_ref[...] = (mid[pl.ds(pl.multiple_of(c * reqs, reqs), reqs), :] + moe).astype(BF16)

    for copy in sends:
        copy.wait_send()
    for i in range(plane):
        to = lax.rem(d + i, plane)

        def sum_sent(to=to):
            pltpu.make_async_remote_copy(
                src_ref=sc,
                dst_ref=rc.at[g, col_half],
                send_sem=send_c.at[to],
                recv_sem=recv_c.at[g, col_half],
                device_id=at(lax.div(to, n_cuts), row_block, lax.rem(to, n_cuts)),
                device_id_type=MESH,
            ).wait_send()

        if i == 0:
            pl.when(row_block != g)(sum_sent)
        else:
            sum_sent()

    def sent(i, carry):
        other_of(i).wait_send()
        return carry

    lax.fori_loop(1, flank, sent, 0)


def up_to(value, by):
    return -(-value // by) * by


def fused_fits(queries, cache_keys, residual_in, expert_gate, adapter_in, router, routes, sinks):
    n_side, n_group, n_cuts = (lax.axis_size(name) for name in ("side", "group", "cuts"))
    reqs, width = residual_in.shape
    blk = width // n_group
    heads = sinks.shape[0]
    return (
        n_group == n_cuts
        and n_side == 2
        and n_group == QUARTERS
        and cache_keys.shape[1] == 1
        and expert_gate.shape[1] == FF
        and router.shape[1] == n_side * n_group * n_cuts
        and width % (n_group * QUARTERS) == 0
        and blk % 16 == 0
        and reqs == 16
        and CAP * n_group == 16
        and heads == 8
        and 3 * width * up_to(FF, 128) * 2 <= 50 * 2**20
    )


def fused(
    queries,
    cache_keys,
    cache_values,
    new_keys,
    new_values,
    lengths,
    head_sinks,
    attn_proj,
    residual_in,
    norm_gain,
    router,
    expert_routes,
    expert_gate,
    expert_up,
    expert_down,
    adapter_in,
    adapter_gate,
    adapter_up,
):
    n_side, n_group, n_cuts = (lax.axis_size(name) for name in ("side", "group", "cuts"))
    reqs, width = residual_in.shape
    ff = expert_gate.shape[1]
    heads, hd, cache = head_sinks.shape[0], cache_keys.shape[2], cache_keys.shape[3]
    blk = width // n_group
    half = up_to(-(-blk // 2), 128)
    experts, topk = router.shape[1], expert_routes.shape[1]
    plane = n_side * n_cuts
    pack = n_group * CAP
    lanes = up_to(blk // QUARTERS, 128)
    sizes = (n_side, n_group, n_cuts, reqs, heads, hd, width, ff, blk, experts, topk, half)
    squeezed = (reqs, hd, cache)
    operands = (
        queries,
        new_keys,
        new_values,
        cache_keys.reshape(squeezed),
        cache_values.reshape(squeezed),
        attn_proj.T,
        residual_in,
        norm_gain,
        router.T,
        expert_routes.T,
        expert_gate,
        expert_up,
        expert_down,
        adapter_in.T,
        adapter_gate,
        adapter_up,
    )
    dma = pltpu.SemaphoreType.DMA
    any_space = pl.BlockSpec(memory_space=pl.ANY)
    smem = pl.BlockSpec(memory_space=pltpu.SMEM)
    scratch = [pltpu.VMEM(x.shape, x.dtype) for x in operands]
    scratch += [
        pltpu.VMEM((n_group, reqs, heads * hd), BF16),
        pltpu.VMEM((n_group * reqs, 2 * half), BF16),
        pltpu.VMEM((plane, reqs, half), BF16),
        pltpu.VMEM((reqs, half), BF16),
        pltpu.VMEM((n_group, 2, reqs, half), BF16),
        pltpu.VMEM((n_group * reqs, 2 * half), BF16),
        pltpu.VMEM((n_group, experts + adapter_in.shape[1], blk), BF16),
        pltpu.VMEM((n_group * reqs, blk), F32),
        pltpu.VMEM((n_group, pack, 2 * half), BF16),
        pltpu.VMEM((n_group, pack, 2 * half), BF16),
        pltpu.VMEM((n_group * pack, 2 * half), BF16),
        pltpu.VMEM((2, pack, ff), F32),
        pltpu.VMEM((pack, ff), BF16),
        pltpu.VMEM((pack, width), F32),
        pltpu.VMEM((QUARTERS * pack, lanes), BF16),
        pltpu.VMEM((n_cuts, n_group, QUARTERS * CAP, lanes), BF16),
        pltpu.VMEM((n_group * n_cuts, QUARTERS * CAP, lanes), BF16),
        pltpu.VMEM((QUARTERS * reqs, lanes), BF16),
        pltpu.VMEM((QUARTERS * reqs, lanes), BF16),
        dma((13,)),
        dma((3, n_group)),
        dma((n_group,)),
        dma((n_group,)),
        dma((plane,)),
        dma((plane,)),
        dma((plane,)),
        dma((n_group, 2)),
        dma((n_group,)),
        dma((n_group,)),
        dma((n_group * n_cuts,)),
        dma((n_group * n_cuts,)),
        dma((1,)),
        dma((1,)),
    ]
    return pl.pallas_call(
        functools.partial(layer_kernel, sizes),
        out_shape=jax.ShapeDtypeStruct((reqs, blk), BF16),
        in_specs=[smem, smem] + [any_space] * len(operands),
        out_specs=pl.BlockSpec(memory_space=pltpu.VMEM),
        scratch_shapes=scratch,
        compiler_params=pltpu.CompilerParams(
            collective_id=0, has_side_effects=True, vmem_limit_bytes=62 * 2**20
        ),
        cost_estimate=pl.CostEstimate(
            flops=6 * pack * width * ff, bytes_accessed=6 * width * ff, transcendentals=0
        ),
    )(lengths, head_sinks, *operands)


def shards(
    queries,
    cache_keys,
    cache_values,
    new_keys,
    new_values,
    lengths,
    head_sinks,
    attn_proj,
    residual_in,
    norm_gain,
    router,
    expert_routes,
    expert_gate,
    expert_up,
    expert_down,
    adapter_in,
    adapter_gate,
    adapter_up,
):
    if fused_fits(
        queries,
        cache_keys,
        residual_in,
        expert_gate,
        adapter_in,
        router,
        expert_routes,
        head_sinks,
    ):
        return fused(
            queries,
            cache_keys,
            cache_values,
            new_keys,
            new_values,
            lengths,
            head_sinks,
            attn_proj,
            residual_in,
            norm_gain,
            router,
            expert_routes,
            expert_gate,
            expert_up,
            expert_down,
            adapter_in,
            adapter_gate,
            adapter_up,
        )
    n_group = lax.axis_size("group")
    n_cuts = lax.axis_size("cuts")
    side_index = lax.axis_index("side")
    cut_index = lax.axis_index("cuts")
    attn_out = attention_rows(
        queries, cache_keys, cache_values, new_keys, new_values, lengths, head_sinks
    )
    req_count = attn_out.shape[0]
    width = residual_in.shape[1]
    quarter = width // n_cuts
    partial_cols = jnp.dot(
        lax.all_gather(attn_out, "group", axis=0, tiled=True),
        attn_proj,
        preferred_element_type=jnp.float32,
    )
    partial_rows = lax.all_to_all(
        partial_cols.astype(jnp.bfloat16), "group", split_axis=0, concat_axis=1, tiled=True
    ).astype(partial_cols.dtype)
    projected = lax.psum(partial_rows.astype(jnp.bfloat16), ("side", "cuts")).astype(jnp.float32)
    middle = residual_in.astype(jnp.float32) + projected
    inverse = lax.rsqrt(jnp.mean(middle * middle, axis=1, keepdims=True) + epsilon)
    normed = (middle * inverse * norm_gain).astype(jnp.bfloat16)
    logits = jnp.dot(normed, router, preferred_element_type=jnp.float32)
    expert_count = router.shape[1]
    chosen = (
        expert_routes[:, :, None] == lax.broadcasted_iota(jnp.int32, (1, 1, expert_count), 2)
    ).astype(jnp.float32)
    picked = jnp.sum(chosen * logits[:, None, :], axis=2)
    raw_gate = jax.nn.sigmoid(picked)
    gate_weights = raw_gate / jnp.sum(raw_gate, axis=1, keepdims=True)
    member = jnp.sum(chosen, axis=1)
    earlier = (
        lax.broadcasted_iota(jnp.int32, (req_count, req_count), 1)
        < lax.broadcasted_iota(jnp.int32, (req_count, req_count), 0)
    ).astype(jnp.float32)
    before = jnp.sum(earlier[:, :, None] * member[None, :, :], axis=1)
    slot_pos = jnp.sum(chosen * before[:, None, :], axis=2).astype(jnp.int32)
    slice_width = expert_gate.shape[1]
    local_count = max(slice_width // FF, 1)
    hidden_local = min(slice_width, FF)
    rank_width = adapter_in.shape[1]
    dest_groups = lax.broadcasted_iota(jnp.int32, (n_group, 1), 0)
    row_base = (side_index * n_group + dest_groups) * n_cuts
    local_table = (row_base + cut_index) * slice_width // FF + lax.broadcasted_iota(
        jnp.int32, (1, local_count), 1
    )
    ones_weight = jnp.ones(gate_weights.shape, jnp.float32)
    gate_cols = expert_gate.reshape(width, local_count, hidden_local)
    up_cols = expert_up.reshape(width, local_count, hidden_local)
    down_rows = expert_down.reshape(local_count, hidden_local, width)
    adapt_gate = adapter_gate.reshape(rank_width, local_count, hidden_local)
    adapt_up = adapter_up.reshape(rank_width, local_count, hidden_local)
    placement = routing_matrix(local_table, expert_routes, slot_pos, ones_weight).astype(
        jnp.bfloat16
    )
    outgoing = jnp.einsum(
        "gjcr,rd->gjcd", placement, normed, preferred_element_type=jnp.float32
    ).astype(jnp.bfloat16)
    row_block = lax.all_to_all(outgoing, "group", split_axis=0, concat_axis=0, tiled=True)
    pre_gate = jnp.einsum(
        "gjcd,djh->gjch", row_block, gate_cols, preferred_element_type=jnp.float32
    )
    pre_up = jnp.einsum("gjcd,djh->gjch", row_block, up_cols, preferred_element_type=jnp.float32)
    low_code = jnp.einsum(
        "gjcd,dr->gjcr", row_block, adapter_in, preferred_element_type=jnp.float32
    ).astype(jnp.bfloat16)
    finish_pre_gate = pre_gate
    finish_pre_up = pre_up
    finish_pre_gate = finish_pre_gate + jnp.einsum(
        "gjcr,rjh->gjch", low_code, adapt_gate, preferred_element_type=jnp.float32
    )
    finish_pre_up = finish_pre_up + jnp.einsum(
        "gjcr,rjh->gjch", low_code, adapt_up, preferred_element_type=jnp.float32
    )
    activated = (
        (finish_pre_up + 1.0) * finish_pre_gate * jax.nn.sigmoid(1.702 * finish_pre_gate)
    ).astype(jnp.bfloat16)
    partial_value = jnp.einsum(
        "gjch,jhd->gjcd", activated, down_rows, preferred_element_type=jnp.float32
    )
    returned = lax.all_to_all(
        partial_value.astype(jnp.bfloat16), "group", split_axis=0, concat_axis=0, tiled=True
    ).astype(partial_value.dtype)
    weighting = routing_matrix(local_table, expert_routes, slot_pos, gate_weights)
    moe_part = jnp.einsum("gjcr,gjcd->rd", weighting, returned, precision=lax.Precision.HIGHEST)
    moe_cols = lax.psum_scatter(
        moe_part.astype(jnp.bfloat16), "cuts", scatter_dimension=1, tiled=True
    )
    moe_total = lax.psum(moe_cols, "side").astype(jnp.float32)
    middle_cols = lax.dynamic_slice_in_dim(middle, cut_index * quarter, quarter, 1)
    return (middle_cols + moe_total).astype(jnp.bfloat16)


def solution(mesh):
    placed = (
        P("group", ("side", "cuts")),
        P("group", ("side", "cuts"), None, None),
        P("group", ("side", "cuts"), None, None),
        P("group", ("side", "cuts")),
        P("group", ("side", "cuts")),
        P("group"),
        P(("side", "cuts")),
        P(("side", "cuts"), "group"),
        P("group", None),
        P(),
        P(),
        P("group", None),
        P(None, ("side", "group", "cuts")),
        P(None, ("side", "group", "cuts")),
        P(("side", "group", "cuts"), None),
        P(),
        P(None, ("side", "group", "cuts")),
        P(None, ("side", "group", "cuts")),
    )
    return jax.shard_map(
        shards, mesh=mesh, in_specs=placed, out_specs=P("group", "cuts"), check_vma=False
    )
```
